768 devices in a mesh: etp: 8 (over y), ep: 96 (over z, x, core).
Axes of the slice: x: 4, y: 8, z: 12, core: 2. Of those that a mesh axis runs over, the one named last changes fastest.
Arguments:
- tokens: bfloat16 [1536, 4096], P('ep', 'etp'), may hold values from -6 to 6
- routes: int32 [1536, 8], P('ep'), may hold values from 0 to 95, all different within a row; in each aligned block of 16 rows (0 to 15, 16 to 31, ...) at most 2 rows name the same one
- route_weight: float32 [1536, 8], P('ep'), may hold values from 0.1 to 1
- grad_out: bfloat16 [1536, 4096], P('ep', 'etp'), may hold values from -6 to 6
- w_gate: bfloat16 [96, 4096, 1536], P('ep', None, 'etp'), may hold values from -0.09375 to 0.09375
- w_up: bfloat16 [96, 4096, 1536], P('ep', None, 'etp'), may hold values from -0.09375 to 0.09375
- w_down: bfloat16 [96, 1536, 4096], P('ep', 'etp'), may hold values from -0.15625 to 0.15625
Outputs:
- mixed: bfloat16 [1536, 4096], P('ep', 'etp')
- grad_tokens: bfloat16 [1536, 4096], P('ep', 'etp')
The draws below stay inside these ranges and needn't reach their ends.
Inputs may be any that keep to these rules, and one draw needn't show every extreme that they name: `routes`: each row names 8 different experts. Among the rows of one index of ep, no expert is named more than 2 times, a bound that some block reaches.
All inputs are finite; a program needn't handle non-finite values.
Results may differ from the reference program's by a relative error of at most 0.0064.
Values may be sent and summed in bfloat16 or wider, within the bound.
No kernel may reach another device: no remote copies, remote signals or barrier semaphores. Data moves between devices by JAX's collectives and lax.ppermute only.
A program may use at most 64 MiB of HBM per device.

```python
import math
import jax
import jax.numpy as jnp
import numpy as np
from jax import lax

D = 4096
FF = 1536
TOP = 8
TOK_DEV = 16
TOKENS = 1536
EXPERTS = 96
MOST = 2
SLOTS = 192
N_EP = 96


def block_levels(rng, dims, shards, least, largest):
    def one(position, parts):
        draws = jax.random.uniform(jax.random.fold_in(jax.random.fold_in(rng, 6), position), (parts,), jnp.float32, least / len(shards), largest / len(shards))
        return jnp.repeat(jnp.exp(draws), dims[position] // parts).reshape((-1,) + (1,) * (len(dims) - position - 1))

    factor_of = one(*shards[0])
    for cut in shards[1:]:
        factor_of = factor_of * one(*cut)
    return factor_of


def routed_block(own_key, own, number, rows, count, top, reach, lean):
    sequence = jax.random.permutation(own_key, count)
    heavy_load, ordinary = portions_of(count, rows * top, reach, lean, True), portions_of(count, rows * top, reach, lean, False)
    places = jnp.arange(count)

    def named(sizes, rotation):
        used = int((sizes > 0).sum())
        fixed = max(1, used // 4)
        moved = fixed + (places - fixed + rotation * (used - fixed)) % max(1, count - fixed)
        return jnp.zeros((count,), jnp.int32).at[sequence[jnp.where(places < fixed, places, moved)]].set(jnp.asarray(sizes, jnp.int32))

    sizes = jnp.where(number % 4 == 0, named(heavy_load, number // 4), named(ordinary, number - number // 4 - 1))
    mixed = jax.random.permutation(jax.random.fold_in(own, 3), count)
    giver, taker = mixed[0:count // 2 * 2:2], mixed[1:count // 2 * 2:2]
    room = jnp.minimum(sizes[giver] - 1, reach - sizes[taker]) // 2
    room = jnp.where((giver == sequence[0]) | (taker == sequence[0]) | (sizes[taker] == 0), 0, jnp.maximum(room, 0))
    moved = jax.random.randint(jax.random.fold_in(own, 4), (count // 2,), 0, 1 << 20) % (room + 1)
    sizes = sizes.at[giver].add(-moved).at[taker].add(moved)
    items = jnp.searchsorted(jnp.cumsum(sizes), jnp.arange(rows * top), side="right").astype(jnp.int32)
    grid = items.reshape(top, rows).T
    grid = grid[jax.random.permutation(jax.random.fold_in(own, 1), rows)]
    rotation = jax.random.randint(jax.random.fold_in(own, 2), (rows, 1), 0, top)
    return jnp.take_along_axis(grid, (jnp.arange(top)[None, :] + rotation) % top, axis=1)


def portions_of(amount, total, bound, skew, full):
    loads = [(1 << 20) // math.isqrt(grade ** skew) + 1 for grade in range(1, amount + 1)]
    largest = bound if full else min(bound, max(-(-total // amount), total * loads[0] // sum(loads)))
    least = 1 if total - largest >= amount - 1 else 0
    given, surplus = [largest] + [least] * (amount - 1), total - largest - least * (amount - 1)
    while surplus > 0:
        movable = [i for i in range(1, amount) if given[i] < largest] or [i for i in range(1, amount) if given[i] < bound]
        pool, left = sum([loads[i] for i in movable]), surplus
        for i in movable:
            more = min(bound - given[i], max(1, left * loads[i] // pool), surplus)
            given[i] = given[i] + more
            surplus = surplus - more
    return np.array(given)


def noise(stream_key, dims, deviation, bound, pieces=(), held_as=jnp.bfloat16):
    drawn = deviation * jax.random.normal(stream_key, dims, jnp.float32)
    if pieces:
        drawn = drawn * block_levels(stream_key, dims, pieces, -0.22, 0.18)
    return jnp.clip(drawn, -bound, bound).astype(held_as)


def setup_inputs(seed: int = 0) -> dict:
    key_of = jax.random.split(jax.random.key(seed), 8)
    tokens = noise(key_of[0], (TOKENS, D), 1.0, 6.0, ((0, 96), (1, 8)))
    routes_keys = jax.random.split(jax.random.fold_in(key_of[1], 1), TOKENS // TOK_DEV)
    routes_turns = jax.random.permutation(jax.random.fold_in(key_of[1], 3), TOKENS // TOK_DEV)
    routes = jax.vmap(lambda own, number: routed_block(jax.random.fold_in(key_of[1], 2), own, number, TOK_DEV, EXPERTS, TOP, MOST, 2))(routes_keys, routes_turns).reshape((TOKENS, TOP))
    route_weight = jnp.clip(0.1 + 0.9 * jax.random.uniform(key_of[2], (TOKENS, TOP), jnp.float32) ** block_levels(key_of[2], (TOKENS, TOP), ((0, 96),), -0.2, 0.2), 0.1, 1.0)
    grad_out = noise(key_of[3], (TOKENS, D), 1.0, 6.0, ((0, 96), (1, 8)))
    w_gate = noise(key_of[4], (EXPERTS, D, FF), D ** -0.5, 0.09375, ((0, 96), (2, 8)))
    w_up = noise(key_of[5], (EXPERTS, D, FF), D ** -0.5, 0.09375, ((0, 96), (2, 8)))
    w_down = noise(key_of[6], (EXPERTS, FF, D), FF ** -0.5, 0.15625, ((0, 96), (1, 8)))
    return {"tokens": tokens, "routes": routes, "route_weight": route_weight, "grad_out": grad_out, "w_gate": w_gate, "w_up": w_up, "w_down": w_down}


def expert_pass(operands):
    token_slots, grad_slots, gate_weight, up_weight, down_weight = operands
    gate_pre = jnp.dot(token_slots, gate_weight, preferred_element_type=jnp.float32)
    up_pre = jnp.dot(token_slots, up_weight, preferred_element_type=jnp.float32)
    squash = jax.nn.sigmoid(gate_pre)
    active = gate_pre * squash
    hidden = (active * up_pre).astype(jnp.bfloat16)
    out_slots = jnp.dot(hidden, down_weight, preferred_element_type=jnp.float32).astype(jnp.bfloat16)
    hidden_grad = jnp.dot(grad_slots, down_weight.T, preferred_element_type=jnp.float32)
    up_grad = (hidden_grad * active).astype(jnp.bfloat16)
    gate_grad = (hidden_grad * up_pre * squash * (1.0 + gate_pre * (1.0 - squash))).astype(jnp.bfloat16)
    input_part = jnp.dot(gate_grad, gate_weight.T, preferred_element_type=jnp.float32)
    input_part = input_part + jnp.dot(up_grad, up_weight.T, preferred_element_type=jnp.float32)
    return out_slots, input_part.astype(jnp.bfloat16)


def reference(tokens, routes, route_weight, grad_out, w_gate, w_up, w_down):
    pair_count = TOKENS * TOP
    chosen = routes.reshape(-1).astype(jnp.int32)
    blocks = chosen.reshape(N_EP, TOK_DEV * TOP)
    onehot = (blocks[:, :, None] == jnp.arange(EXPERTS, dtype=jnp.int32)[None, None, :]).astype(jnp.int32)
    earlier = jnp.cumsum(onehot, axis=1) - onehot
    within = jnp.sum(earlier * onehot, axis=2)
    source = jnp.arange(N_EP, dtype=jnp.int32)[:, None]
    slot_index = (source * MOST + within).reshape(-1).astype(jnp.int32)
    token_index = (jnp.arange(pair_count, dtype=jnp.int32) // TOP).astype(jnp.int32)
    token_rows = tokens[token_index]
    grad_rows = (route_weight.reshape(-1)[:, None].astype(jnp.float32) * grad_out[token_index].astype(jnp.float32)).astype(jnp.bfloat16)
    token_slots = jnp.zeros((EXPERTS, SLOTS, D), tokens.dtype).at[chosen, slot_index].set(token_rows)
    grad_slots = jnp.zeros((EXPERTS, SLOTS, D), tokens.dtype).at[chosen, slot_index].set(grad_rows)
    out_slots, input_slots = lax.map(expert_pass, (token_slots, grad_slots, w_gate, w_up, w_down))
    out_rows = out_slots[chosen, slot_index].astype(jnp.float32).reshape(TOKENS, TOP, D)
    input_rows = input_slots[chosen, slot_index].astype(jnp.float32).reshape(TOKENS, TOP, D)
    weights = route_weight.astype(jnp.float32)[:, :, None]
    mixed = jnp.sum(weights * out_rows, axis=1).astype(jnp.bfloat16)
    grad_tokens = jnp.sum(input_rows, axis=1).astype(jnp.bfloat16)
    return mixed, grad_tokens
```

```python
import jax
import jax.numpy as jnp
from jax import lax
from jax.sharding import PartitionSpec as P

bf16 = jnp.bfloat16
f32 = jnp.float32


def contract_last(left, right):
    return lax.dot_general(left, right, (((1,), (1,)), ((), ())), preferred_element_type=f32)


def on_device(tokens, routes, route_weight, grad_out, w_gate, w_up, w_down):
    owners = lax.axis_size("ep")
    tok_rows, local_width = tokens.shape
    top_count = routes.shape[1]
    capacity = min(tok_rows, max(2, (3 * tok_rows * top_count + 2 * owners - 1) // (2 * owners)))
    slots = owners * capacity
    chosen = routes.reshape(-1)
    onehot = (chosen[:, None] == jnp.arange(owners, dtype=jnp.int32)[None, :]).astype(jnp.int32)
    earlier = jnp.cumsum(onehot, axis=0) - onehot
    within = jnp.sum(earlier * onehot, axis=1)
    target = chosen * (2 * capacity) + within
    rows = jnp.arange(2 * slots, dtype=jnp.int32)
    pick_token = (rows[:, None] == target[None, :]).astype(bf16)
    pick_grad = (rows[:, None] == target[None, :] + capacity).astype(bf16)
    token_pairs = jnp.repeat(tokens, top_count, axis=0)
    grad_pairs = (
        route_weight.reshape(-1)[:, None] * jnp.repeat(grad_out, top_count, axis=0).astype(f32)
    ).astype(bf16)
    send = jnp.dot(
        jnp.concatenate([pick_token, pick_grad], axis=1),
        jnp.concatenate([token_pairs, grad_pairs], axis=0),
        preferred_element_type=f32,
    ).astype(bf16)
    recv = lax.all_to_all(
        send.reshape(owners, 2 * capacity, local_width), "ep", split_axis=0, concat_axis=0, tiled=True
    ).reshape(2 * slots, local_width)
    place = jnp.arange(2 * slots, dtype=jnp.int32)
    kind, slot = place // slots, place % slots
    source = (slot // capacity) * (2 * capacity) + kind * capacity + slot % capacity
    sort = (source[:, None] == rows[None, :]).astype(bf16)
    sorted_rows = jnp.dot(sort, recv, preferred_element_type=f32).astype(bf16)
    full = lax.all_gather(sorted_rows, "etp", axis=1, tiled=True)
    token_slots, grad_slots = full[:slots], full[slots:]
    gate_weight, up_weight, down_weight = w_gate[0], w_up[0], w_down[0]
    gate_pre = jnp.dot(token_slots, gate_weight, preferred_element_type=f32)
    up_pre = jnp.dot(token_slots, up_weight, preferred_element_type=f32)
    squash = jax.nn.sigmoid(gate_pre)
    active = gate_pre * squash
    hidden = (active * up_pre).astype(bf16)
    hidden_grad = contract_last(grad_slots, down_weight)
    up_grad = (hidden_grad * active).astype(bf16)
    gate_grad = (hidden_grad * up_pre * squash * (1.0 + gate_pre * (1.0 - squash))).astype(bf16)
    out_part = jnp.dot(hidden, down_weight, preferred_element_type=f32)
    input_part = contract_last(gate_grad, gate_weight) + contract_last(up_grad, up_weight)
    part = jnp.concatenate([out_part.astype(bf16), input_part.astype(bf16)], axis=0)
    local = lax.psum_scatter(part, "etp", scatter_dimension=1, tiled=True)
    unsorted = lax.dot_general(
        sort, local, (((0,), (0,)), ((), ())), preferred_element_type=f32
    ).astype(bf16)
    back = lax.all_to_all(
        unsorted.reshape(owners, 2 * capacity, local_width), "ep", split_axis=0, concat_axis=0, tiled=True
    ).reshape(2 * slots, local_width)
    first = (((0,), (0,)), ((), ()))
    out_rows = lax.dot_general(pick_token, back, first, preferred_element_type=f32)
    input_rows = lax.dot_general(pick_grad, back, first, preferred_element_type=f32)
    out_rows = out_rows.reshape(tok_rows, top_count, local_width)
    input_rows = input_rows.reshape(tok_rows, top_count, local_width)
    mixed = jnp.sum(route_weight[:, :, None] * out_rows, axis=1).astype(bf16)
    grad_tokens = jnp.sum(input_rows, axis=1).astype(bf16)
    return (mixed, grad_tokens)


def solution(mesh):
    in_specs = (
        P("ep", "etp"),
        P("ep", None),
        P("ep", None),
        P("ep", "etp"),
        P("ep", None, "etp"),
        P("ep", None, "etp"),
        P("ep", "etp", None),
    )
    out_specs = (P("ep", "etp"), P("ep", "etp"))
    return jax.shard_map(
        on_device, mesh=mesh, in_specs=in_specs, out_specs=out_specs, check_vma=False
    )
```

```python
import jax
import jax.numpy as jnp
from jax import lax
from jax.experimental import pallas as pl
from jax.experimental.pallas import tpu as pltpu
from jax.sharding import PartitionSpec as P

bf16 = jnp.bfloat16
f32 = jnp.float32
VMEM = pl.BlockSpec(memory_space=pltpu.VMEM)
VMEM_LIMIT = 28 * 1024 * 1024


def dot_last(left, right):
    return lax.dot_general(left, right, (((1,), (1,)), ((), ())), preferred_element_type=f32)


def dot(left, right):
    return lax.dot_general(left, right, (((1,), (0,)), ((), ())), preferred_element_type=f32)


def exchange(value, step):
    size, owners = lax.axis_size("etp"), lax.axis_size("ep")
    pairs = []
    for y in range(size):
        for j in range(owners):
            sign = 1 if (y + j + step) % 2 == 0 else -1
            pairs.append((y * owners + j, (y + sign) % size * owners + j))
    return lax.ppermute(value, ("etp", "ep"), pairs)


def gather_step(held, step):
    if step == 0:
        return [jnp.stack([held[0], exchange(held[0], 0)])]
    return held + [exchange(held[-1], step)]


def columns_of(steps, width):
    size = 2 * steps
    y = lax.axis_index("etp")
    sign = 1 - 2 * lax.rem(y + lax.axis_index("ep"), 2)
    out = []
    for k in range(steps):
        turn = sign if k % 2 == 0 else -sign
        blocks = [lax.rem(y + turn * (k + b) + 2 * size, size) for b in (0, 1)]
        out.append([pl.ds(pl.multiple_of(block * width, width), width) for block in blocks])
    return out


def forward_kernel(steps, *refs):
    held, (gate_w, up_w, down_w) = refs[:steps], refs[steps : steps + 3]
    gate_ref, up_ref = refs[steps + 3 : steps + 5]
    parts = refs[steps + 5 :]
    columns = columns_of(steps, held[0].shape[2])
    gate = up = None
    for k in range(steps):
        for b in (0, 1):
            rows = held[k][b]
            gate_now = dot_last(rows, gate_w[:, columns[k][b]])
            up_now = dot_last(rows, up_w[:, columns[k][b]])
            gate = gate_now if gate is None else gate + gate_now
            up = up_now if up is None else up + up_now
    gate_ref[...] = gate
    up_ref[...] = up
    hidden = (gate * jax.nn.sigmoid(gate) * up).astype(bf16)
    for k in reversed(range(steps)):
        for b in (0, 1):
            parts[k][b] = dot(hidden, down_w[:, columns[k][b]]).astype(parts[k].dtype)


def backward_kernel(steps, *refs):
    held, (gate_w, up_w, down_w) = refs[:steps], refs[steps : steps + 3]
    gate_ref, up_ref = refs[steps + 3 : steps + 5]
    parts = refs[steps + 5 :]
    columns = columns_of(steps, held[0].shape[2])
    hidden_grad = None
    for k in range(steps):
        for b in (0, 1):
            now = dot_last(held[k][b], down_w[:, columns[k][b]])
            hidden_grad = now if hidden_grad is None else hidden_grad + now
    gate, up = gate_ref[...], up_ref[...]
    squash = jax.nn.sigmoid(gate)
    up_grad = (hidden_grad * (gate * squash)).astype(bf16)
    gate_grad = (hidden_grad * up * squash * (1.0 + gate * (1.0 - squash))).astype(bf16)
    for k in reversed(range(steps)):
        for b in (0, 1):
            part = dot(gate_grad, gate_w[:, columns[k][b]]) + dot(up_grad, up_w[:, columns[k][b]])
            parts[k][b] = part.astype(parts[k].dtype)


def call(kernel, steps, operands, extra_shapes, pair_shape, flops):
    shapes = extra_shapes + [
        jax.ShapeDtypeStruct(pair_shape, f32 if k < steps - 1 else bf16) for k in range(steps)
    ]
    return pl.pallas_call(
        lambda *refs: kernel(steps, *refs),
        out_shape=shapes,
        in_specs=[VMEM] * len(operands),
        out_specs=[VMEM] * len(shapes),
        compiler_params=pltpu.CompilerParams(vmem_limit_bytes=VMEM_LIMIT),
        cost_estimate=pl.CostEstimate(flops=flops, bytes_accessed=9 << 20, transcendentals=0),
    )(*operands)


def sum_step(parts, arrived, step):
    received = exchange(arrived, step)
    return (parts[step - 1] + received.astype(f32)).astype(bf16)


def on_device(tokens, routes, route_weight, grad_out, w_gate, w_up, w_down):
    owners, steps = lax.axis_size("ep"), lax.axis_size("etp") // 2
    tok_rows, local_width = tokens.shape
    top_count = routes.shape[1]
    capacity = min(tok_rows, max(2, (3 * tok_rows * top_count + 2 * owners - 1) // (2 * owners)))
    slots = owners * capacity
    chosen = routes.reshape(-1)
    onehot = (chosen[:, None] == jnp.arange(owners, dtype=jnp.int32)[None, :]).astype(jnp.int32)
    earlier = jnp.cumsum(onehot, axis=0) - onehot
    within = jnp.sum(earlier * onehot, axis=1)
    target = chosen * (2 * capacity) + within
    rows = jnp.arange(2 * slots, dtype=jnp.int32)
    pick_token = (rows[:, None] == target[None, :]).astype(bf16)
    pick_grad = (rows[:, None] == target[None, :] + capacity).astype(bf16)
    token_pairs = jnp.repeat(tokens, top_count, axis=0)
    grad_pairs = (
        route_weight.reshape(-1)[:, None] * jnp.repeat(grad_out, top_count, axis=0).astype(f32)
    ).astype(bf16)
    send = jnp.dot(
        jnp.concatenate([pick_token, pick_grad], axis=1),
        jnp.concatenate([token_pairs, grad_pairs], axis=0),
        preferred_element_type=f32,
    ).astype(bf16)
    recv = lax.all_to_all(
        send.reshape(owners, 2 * capacity, local_width), "ep", split_axis=0, concat_axis=0, tiled=True
    ).reshape(2 * slots, local_width)
    place = jnp.arange(2 * slots, dtype=jnp.int32)
    kind, slot = place // slots, place % slots
    source = (slot // capacity) * (2 * capacity) + kind * capacity + slot % capacity
    sort = (source[:, None] == rows[None, :]).astype(bf16)
    token_held = [jnp.dot(sort[:slots], recv, preferred_element_type=f32).astype(bf16)]
    grad_held = [jnp.dot(sort[slots:], recv, preferred_element_type=f32).astype(bf16)]
    for step in range(steps):
        token_held = gather_step(token_held, step)
        grad_held = gather_step(grad_held, step)
    gate_weight, up_weight, down_weight = w_gate[0].T, w_up[0].T, w_down[0]
    weights = [gate_weight, up_weight, down_weight]
    hidden_width, width = down_weight.shape
    square = jax.ShapeDtypeStruct((slots, hidden_width), f32)
    pair_shape = (2, slots, local_width)
    flops = 2 * slots * hidden_width * width
    gate, up, *out_parts = call(
        forward_kernel, steps, token_held + weights, [square, square], pair_shape, 3 * flops
    )
    input_parts = call(
        backward_kernel, steps, grad_held + weights + [gate, up], [], pair_shape, 3 * flops
    )
    out_sum, input_sum = out_parts[-1], input_parts[-1]
    for step in reversed(range(1, steps)):
        out_sum = sum_step(out_parts, out_sum, step)
        input_sum = sum_step(input_parts, input_sum, step)
    out_local = (out_sum[0].astype(f32) + exchange(out_sum[1], 0).astype(f32)).astype(bf16)
    input_local = (input_sum[0].astype(f32) + exchange(input_sum[1], 0).astype(f32)).astype(bf16)
    local = jnp.concatenate([out_local, input_local], axis=0)
    unsorted = lax.dot_general(
        sort, local, (((0,), (0,)), ((), ())), preferred_element_type=f32
    ).astype(bf16)
    back = lax.all_to_all(
        unsorted.reshape(owners, 2 * capacity, local_width), "ep", split_axis=0, concat_axis=0, tiled=True
    ).reshape(2 * slots, local_width)
    first = (((0,), (0,)), ((), ()))
    out_rows = lax.dot_general(pick_token, back, first, preferred_element_type=f32)
    input_rows = lax.dot_general(pick_grad, back, first, preferred_element_type=f32)
    out_rows = out_rows.reshape(tok_rows, top_count, local_width)
    input_rows = input_rows.reshape(tok_rows, top_count, local_width)
    mixed = jnp.sum(route_weight[:, :, None] * out_rows, axis=1).astype(bf16)
    grad_tokens = jnp.sum(input_rows, axis=1).astype(bf16)
    return (mixed, grad_tokens)


def solution(mesh):
    in_specs = (
        P("ep", "etp"),
        P("ep", None),
        P("ep", None),
        P("ep", "etp"),
        P("ep", None, "etp"),
        P("ep", None, "etp"),
        P("ep", "etp", None),
    )
    out_specs = (P("ep", "etp"), P("ep", "etp"))
    return jax.shard_map(
        on_device, mesh=mesh, in_specs=in_specs, out_specs=out_specs, check_vma=False
    )
```

```python
import jax
import jax.numpy as jnp
from jax import lax
from jax.experimental import pallas as pl
from jax.experimental.pallas import tpu as pltpu
from jax.sharding import PartitionSpec as P

bf16 = jnp.bfloat16
f32 = jnp.float32
VMEM = pl.BlockSpec(memory_space=pltpu.VMEM)
VMEM_LIMIT = 28 * 1024 * 1024


def dot_last(left, right):
    return lax.dot_general(left, right, (((1,), (1,)), ((), ())), preferred_element_type=f32)


def dot(left, right):
    return lax.dot_general(left, right, (((1,), (0,)), ((), ())), preferred_element_type=f32)


def split3(value):
    high = value.astype(bf16)
    rest = value - high.astype(f32)
    middle = rest.astype(bf16)
    return high, middle, (rest - middle.astype(f32)).astype(bf16)


def dot_first(left, right):
    return lax.dot_general(left, right, (((0,), (0,)), ((), ())), preferred_element_type=f32)


def travel_row(slot, kind, capacity):
    return lax.div(slot, capacity) * (2 * capacity) + kind * capacity + lax.rem(slot, capacity)


def picks(capacity, routes, weight, rows):
    shape = (rows, routes.shape[1])
    row = lax.broadcasted_iota(jnp.int32, shape, 0)
    owner = lax.div(row, 2 * capacity)
    named = jnp.zeros(shape, f32)
    scale = jnp.zeros(shape, f32)
    for k in range(routes.shape[0]):
        hit = routes[k : k + 1, :] == owner
        named = jnp.where(hit, 1.0, named)
        scale = jnp.where(hit, weight[k : k + 1, :], scale)
    square = (shape[1], shape[1])
    before = lax.broadcasted_iota(jnp.int32, square, 0) < lax.broadcasted_iota(jnp.int32, square, 1)
    earlier = dot(named.astype(bf16), before.astype(f32).astype(bf16))
    here = earlier == lax.rem(row, capacity).astype(f32)
    gradient = lax.rem(row, 2 * capacity) >= capacity
    return jnp.where(here, named, 0.0), jnp.where(here, scale, 0.0), gradient


def dispatch_kernel(capacity, routes, weight, tokens, grads, send):
    pick, weighted, gradient = picks(capacity, routes, weight, send.shape[0])
    out = dot(jnp.where(gradient, 0.0, pick).astype(bf16), tokens[...])
    for part in split3(jnp.where(gradient, weighted, 0.0)):
        out = out + dot(part, grads[...])
    send[...] = out.astype(bf16)


def sort_kernel(capacity, recv, token_rows, grad_rows):
    rows = recv.shape[0]
    for kind, out in ((0, token_rows), (1, grad_rows)):
        shape = (rows // 2, rows)
        source = travel_row(lax.broadcasted_iota(jnp.int32, shape, 0), kind, capacity)
        place = (source == lax.broadcasted_iota(jnp.int32, shape, 1)).astype(f32).astype(bf16)
        out[...] = dot(place, recv[...]).astype(bf16)


def unsort_kernel(capacity, out_sum, out_last, input_sum, input_last, unsorted):
    rows = unsorted.shape[0]
    total = None
    for kind, held, last in ((0, out_sum, out_last), (1, input_sum, input_last)):
        local = (held[0].astype(f32) + last[...].astype(f32)).astype(bf16)
        shape = (rows, rows // 2)
        target = travel_row(lax.broadcasted_iota(jnp.int32, shape, 1), kind, capacity)
        place = (target == lax.broadcasted_iota(jnp.int32, shape, 0)).astype(f32).astype(bf16)
        now = dot(place, local)
        total = now if total is None else total + now
    unsorted[...] = total.astype(bf16)


def combine_kernel(capacity, routes, weight, back, mixed, grad_tokens):
    pick, weighted, gradient = picks(capacity, routes, weight, back.shape[0])
    rows = back[...]
    out = None
    for part in split3(jnp.where(gradient, 0.0, weighted)):
        now = dot_first(part, rows)
        out = now if out is None else out + now
    mixed[...] = out.astype(bf16)
    grad_tokens[...] = dot_first(jnp.where(gradient, pick, 0.0).astype(bf16), rows).astype(bf16)


def exchange(value, step, chain):
    size, owners = lax.axis_size("etp"), lax.axis_size("ep")
    pairs = []
    for y in range(size):
        for j in range(owners):
            sign = 1 if (y + j + step + chain) % 2 == 0 else -1
            pairs.append((y * owners + j, (y + sign) % size * owners + j))
    return lax.ppermute(value, ("etp", "ep"), pairs)


def columns_of(steps, width, chain):
    size = 2 * steps
    y = lax.axis_index("etp")
    sign = 1 - 2 * lax.rem(y + lax.axis_index("ep") + chain, 2)
    out = []
    for k in range(steps):
        turn = sign if k % 2 == 0 else -sign
        blocks = [lax.rem(y + turn * (k + b) + 2 * size, size) for b in (0, 1)]
        out.append([pl.ds(pl.multiple_of(block * width, width), width) for block in blocks])
    return out


def forward_kernel(steps, *refs):
    held, (gate_w, up_w, down_w) = refs[:steps], refs[steps : steps + 3]
    gate_ref, up_ref = refs[steps + 3 : steps + 5]
    parts = refs[steps + 5 :]
    columns = columns_of(steps, held[0].shape[2], 0)
    gate = up = None
    for k in range(steps):
        for b in (0, 1):
            rows = held[k][b]
            gate_now = dot_last(rows, gate_w[:, columns[k][b]])
            up_now = dot_last(rows, up_w[:, columns[k][b]])
            gate = gate_now if gate is None else gate + gate_now
            up = up_now if up is None else up + up_now
    gate_ref[...] = gate
    up_ref[...] = up
    hidden = (gate * jax.nn.sigmoid(gate) * up).astype(bf16)
    for k in reversed(range(steps)):
        for b in (0, 1):
            parts[k][b] = dot(hidden, down_w[:, columns[k][b]]).astype(parts[k].dtype)


def backward_kernel(steps, *refs):
    held, (gate_w, up_w, down_w) = refs[:steps], refs[steps : steps + 3]
    gate_ref, up_ref = refs[steps + 3 : steps + 5]
    parts = refs[steps + 5 :]
    columns = columns_of(steps, held[0].shape[2], 1)
    hidden_grad = None
    for k in range(steps):
        for b in (0, 1):
            now = dot_last(held[k][b], down_w[:, columns[k][b]])
            hidden_grad = now if hidden_grad is None else hidden_grad + now
    gate, up = gate_ref[...], up_ref[...]
    squash = jax.nn.sigmoid(gate)
    up_grad = (hidden_grad * (gate * squash)).astype(bf16)
    gate_grad = (hidden_grad * up * squash * (1.0 + gate * (1.0 - squash))).astype(bf16)
    for k in reversed(range(steps)):
        for b in (0, 1):
            part = dot(gate_grad, gate_w[:, columns[k][b]]) + dot(up_grad, up_w[:, columns[k][b]])
            parts[k][b] = part.astype(parts[k].dtype)


def call(kernel, steps, operands, extra_shapes, pair_shape, flops):
    shapes = extra_shapes + [
        jax.ShapeDtypeStruct(pair_shape, f32 if k < steps - 1 else bf16) for k in range(steps)
    ]
    return pl.pallas_call(
        lambda *refs: kernel(steps, *refs),
        out_shape=shapes,
        in_specs=[VMEM] * len(operands),
        out_specs=[VMEM] * len(shapes),
        compiler_params=pltpu.CompilerParams(vmem_limit_bytes=VMEM_LIMIT),
        cost_estimate=pl.CostEstimate(flops=flops, bytes_accessed=9 << 20, transcendentals=0),
    )(*operands)


def sum_step(parts, arrived, step, chain):
    received = exchange(arrived, step, chain)
    return (parts[step - 1] + received.astype(f32)).astype(bf16)


def on_device(tokens, routes, route_weight, grad_out, w_gate, w_up, w_down):
    owners, steps = lax.axis_size("ep"), lax.axis_size("etp") // 2
    tok_rows, local_width = tokens.shape
    top_count = routes.shape[1]
    capacity = min(tok_rows, max(2, (3 * tok_rows * top_count + 2 * owners - 1) // (2 * owners)))
    slots = owners * capacity
    rows = 2 * slots
    send = pl.pallas_call(
        lambda *refs: dispatch_kernel(capacity, *refs),
        out_shape=jax.ShapeDtypeStruct((rows, local_width), bf16),
        compiler_params=pltpu.CompilerParams(vmem_limit_bytes=VMEM_LIMIT),
    )(routes.T, route_weight.T, tokens, grad_out)
    recv = lax.all_to_all(
        send.reshape(owners, 2 * capacity, local_width), "ep", split_axis=0, concat_axis=0, tiled=True
    ).reshape(rows, local_width)
    half = jax.ShapeDtypeStruct((slots, local_width), bf16)
    token_rows, grad_rows = pl.pallas_call(
        lambda *refs: sort_kernel(capacity, *refs),
        out_shape=[half, half],
        in_specs=[VMEM],
        out_specs=[VMEM] * 2,
        compiler_params=pltpu.CompilerParams(vmem_limit_bytes=VMEM_LIMIT),
    )(recv)
    token_next, grad_next = lax.optimization_barrier(
        (exchange(token_rows, 0, 0), exchange(grad_rows, 0, 1))
    )
    token_held = [jnp.stack([token_rows, token_next])]
    grad_held = [jnp.stack([grad_rows, grad_next])]
    for step in range(1, steps):
        token_held.append(exchange(token_held[-1], step, 0))
        grad_held.append(exchange(grad_held[-1], step, 1))
    gate_weight, up_weight, down_weight = w_gate[0].T, w_up[0].T, w_down[0]
    weights = [gate_weight, up_weight, down_weight]
    hidden_width, width = down_weight.shape
    square = jax.ShapeDtypeStruct((slots, hidden_width), f32)
    pair_shape = (2, slots, local_width)
    flops = 2 * slots * hidden_width * width
    gate, up, *out_parts = call(
        forward_kernel, steps, token_held + weights, [square, square], pair_shape, 3 * flops
    )
    input_parts = call(
        backward_kernel, steps, grad_held + weights + [gate, up], [], pair_shape, 3 * flops
    )
    out_sum, input_sum = out_parts[-1], input_parts[-1]
    for step in reversed(range(1, steps)):
        out_sum = sum_step(out_parts, out_sum, step, 0)
        input_sum = sum_step(input_parts, input_sum, step, 1)
    unsorted = pl.pallas_call(
        lambda *refs: unsort_kernel(capacity, *refs),
        out_shape=jax.ShapeDtypeStruct((rows, local_width), bf16),
        in_specs=[VMEM] * 4,
        out_specs=VMEM,
        compiler_params=pltpu.CompilerParams(vmem_limit_bytes=VMEM_LIMIT),
    )(out_sum, exchange(out_sum[1], 0, 0), input_sum, exchange(input_sum[1], 0, 1))
    back = lax.all_to_all(
        unsorted.reshape(owners, 2 * capacity, local_width), "ep", split_axis=0, concat_axis=0, tiled=True
    ).reshape(rows, local_width)
    mine = jax.ShapeDtypeStruct((tok_rows, local_width), bf16)
    mixed, grad_tokens = pl.pallas_call(
        lambda *refs: combine_kernel(capacity, *refs),
        out_shape=[mine, mine],
        in_specs=[VMEM] * 3,
        out_specs=[VMEM] * 2,
        compiler_params=pltpu.CompilerParams(vmem_limit_bytes=VMEM_LIMIT),
    )(routes.T, route_weight.T, back)
    return (mixed, grad_tokens)


def solution(mesh):
    in_specs = (
        P("ep", "etp"),
        P("ep", None),
        P("ep", None),
        P("ep", "etp"),
        P("ep", None, "etp"),
        P("ep", None, "etp"),
        P("ep", "etp", None),
    )
    out_specs = (P("ep", "etp"), P("ep", "etp"))
    return jax.shard_map(
        on_device, mesh=mesh, in_specs=in_specs, out_specs=out_specs, check_vma=False
    )
```

```python
import jax
import jax.numpy as jnp
from jax import lax
from jax.experimental import pallas as pl
from jax.experimental.pallas import tpu as pltpu
from jax.sharding import PartitionSpec as P

bf16 = jnp.bfloat16
f32 = jnp.float32
VMEM = pl.BlockSpec(memory_space=pltpu.VMEM)
ANY = pl.BlockSpec(memory_space=pl.ANY)
VMEM_LIMIT = 12 * 1024 * 1024
CHUNKS = 4


def dot_last(left, right):
    return lax.dot_general(left, right, (((1,), (1,)), ((), ())), preferred_element_type=f32)


def dot(left, right):
    return lax.dot_general(left, right, (((1,), (0,)), ((), ())), preferred_element_type=f32)


def split3(value):
    high = value.astype(bf16)
    rest = value - high.astype(f32)
    middle = rest.astype(bf16)
    return high, middle, (rest - middle.astype(f32)).astype(bf16)


def dot_first(left, right):
    return lax.dot_general(left, right, (((0,), (0,)), ((), ())), preferred_element_type=f32)


def travel_row(slot, kind, capacity):
    return lax.div(slot, capacity) * (2 * capacity) + kind * capacity + lax.rem(slot, capacity)


def picks(capacity, routes, weight, rows):
    shape = (rows, routes.shape[1])
    row = lax.broadcasted_iota(jnp.int32, shape, 0)
    owner = lax.div(row, 2 * capacity)
    named = jnp.zeros(shape, f32)
    scale = jnp.zeros(shape, f32)
    for k in range(routes.shape[0]):
        hit = routes[k : k + 1, :] == owner
        named = jnp.where(hit, 1.0, named)
        scale = jnp.where(hit, weight[k : k + 1, :], scale)
    square = (shape[1], shape[1])
    before = lax.broadcasted_iota(jnp.int32, square, 0) < lax.broadcasted_iota(jnp.int32, square, 1)
    earlier = dot(named.astype(bf16), before.astype(f32).astype(bf16))
    here = earlier == lax.rem(row, capacity).astype(f32)
    gradient = lax.rem(row, 2 * capacity) >= capacity
    return jnp.where(here, named, 0.0), jnp.where(here, scale, 0.0), gradient


def dispatch_kernel(capacity, routes, weight, tokens, grads, send):
    pick, weighted, gradient = picks(capacity, routes, weight, send.shape[0])
    out = dot(jnp.where(gradient, 0.0, pick).astype(bf16), tokens[...])
    for part in split3(jnp.where(gradient, weighted, 0.0)):
        out = out + dot(part, grads[...])
    send[...] = out.astype(bf16)


def sort_kernel(capacity, recv, token_rows, grad_rows):
    rows = recv.shape[0]
    for kind, out in ((0, token_rows), (1, grad_rows)):
        shape = (rows // 2, rows)
        source = travel_row(lax.broadcasted_iota(jnp.int32, shape, 0), kind, capacity)
        place = (source == lax.broadcasted_iota(jnp.int32, shape, 1)).astype(f32).astype(bf16)
        out[...] = dot(place, recv[...]).astype(bf16)


def unsort_kernel(capacity, out_sum, out_last, input_local, unsorted):
    rows = unsorted.shape[0]
    out_local = (out_sum[0].astype(f32) + out_last[...].astype(f32)).astype(bf16)
    total = None
    for kind, local in ((0, out_local), (1, input_local[...])):
        shape = (rows, rows // 2)
        target = travel_row(lax.broadcasted_iota(jnp.int32, shape, 1), kind, capacity)
        place = (target == lax.broadcasted_iota(jnp.int32, shape, 0)).astype(f32).astype(bf16)
        now = dot(place, local)
        total = now if total is None else total + now
    unsorted[...] = total.astype(bf16)


def combine_kernel(capacity, routes, weight, back, mixed, grad_tokens):
    pick, weighted, gradient = picks(capacity, routes, weight, back.shape[0])
    rows = back[...]
    out = None
    for part in split3(jnp.where(gradient, 0.0, weighted)):
        now = dot_first(part, rows)
        out = now if out is None else out + now
    mixed[...] = out.astype(bf16)
    grad_tokens[...] = dot_first(jnp.where(gradient, pick, 0.0).astype(bf16), rows).astype(bf16)


def exchange(value, step):
    size, owners = lax.axis_size("etp"), lax.axis_size("ep")
    pairs = []
    for y in range(size):
        for j in range(owners):
            sign = 1 if (y + j + step) % 2 == 0 else -1
            pairs.append((y * owners + j, (y + sign) % size * owners + j))
    return lax.ppermute(value, ("etp", "ep"), pairs)


def columns_of(steps, width):
    size = 2 * steps
    y = lax.axis_index("etp")
    sign = 1 - 2 * lax.rem(y + lax.axis_index("ep"), 2)
    out = []
    for k in range(steps):
        turn = sign if k % 2 == 0 else -sign
        blocks = [lax.rem(y + turn * (k + b) + 2 * size, size) for b in (0, 1)]
        out.append([pl.ds(pl.multiple_of(block * width, width), width) for block in blocks])
    return out


def forward_kernel(steps, *refs):
    held, (gate_w, up_w, down_w) = refs[:steps], refs[steps : steps + 3]
    gate_ref, up_ref = refs[steps + 3 : steps + 5]
    parts = refs[steps + 5 :]
    columns = columns_of(steps, held[0].shape[2])
    gate = up = None
    for k in range(steps):
        for b in (0, 1):
            rows = held[k][b]
            gate_now = dot_last(rows, gate_w[:, columns[k][b]])
            up_now = dot_last(rows, up_w[:, columns[k][b]])
            gate = gate_now if gate is None else gate + gate_now
            up = up_now if up is None else up + up_now
    gate_ref[...] = gate
    up_ref[...] = up
    hidden = (gate * jax.nn.sigmoid(gate) * up).astype(bf16)
    for k in reversed(range(steps)):
        for b in (0, 1):
            parts[k][b] = dot(hidden, down_w[:, columns[k][b]]).astype(parts[k].dtype)


def backward_kernel(rows_hbm, gate_w, up_w, down_w, gate_ref, up_ref, part_hbm, rows, part, in_sem, out_sem):
    chunk = rows.shape[1] // CHUNKS
    columns = [slice(c * chunk, (c + 1) * chunk) for c in range(CHUNKS)]
    arriving = [
        pltpu.make_async_copy(rows_hbm.at[:, columns[c]], rows.at[:, columns[c]], in_sem.at[c])
        for c in range(CHUNKS)
    ]
    for copy in arriving:
        copy.start()
    hidden_grad = None
    for c in range(CHUNKS):
        arriving[c].wait()
        now = dot_last(rows[:, columns[c]], down_w[:, columns[c]])
        hidden_grad = now if hidden_grad is None else hidden_grad + now
    gate, up = gate_ref[...], up_ref[...]
    squash = jax.nn.sigmoid(gate)
    up_grad = (hidden_grad * (gate * squash)).astype(bf16)
    gate_grad = (hidden_grad * up * squash * (1.0 + gate * (1.0 - squash))).astype(bf16)
    leaving = []
    for c in range(CHUNKS):
        now = dot(gate_grad, gate_w[:, columns[c]]) + dot(up_grad, up_w[:, columns[c]])
        part[:, columns[c]] = now.astype(bf16)
        copy = pltpu.make_async_copy(part.at[:, columns[c]], part_hbm.at[:, columns[c]], out_sem.at[c])
        copy.start()
        leaving.append(copy)
    for copy in leaving:
        copy.wait()


def sum_step(parts, arrived, step):
    received = exchange(arrived, step)
    return (parts[step - 1] + received.astype(f32)).astype(bf16)


def on_device(tokens, routes, route_weight, grad_out, w_gate, w_up, w_down):
    owners, steps = lax.axis_size("ep"), lax.axis_size("etp") // 2
    tok_rows, local_width = tokens.shape
    top_count = routes.shape[1]
    capacity = min(tok_rows, max(2, (3 * tok_rows * top_count + 2 * owners - 1) // (2 * owners)))
    slots = owners * capacity
    rows = 2 * slots
    send = pl.pallas_call(
        lambda *refs: dispatch_kernel(capacity, *refs),
        out_shape=jax.ShapeDtypeStruct((rows, local_width), bf16),
        compiler_params=pltpu.CompilerParams(vmem_limit_bytes=VMEM_LIMIT),
    )(routes.T, route_weight.T, tokens, grad_out)
    recv = lax.all_to_all(
        send.reshape(owners, 2 * capacity, local_width), "ep", split_axis=0, concat_axis=0, tiled=True
    ).reshape(rows, local_width)
    half = jax.ShapeDtypeStruct((slots, local_width), bf16)
    token_rows, grad_rows = pl.pallas_call(
        lambda *refs: sort_kernel(capacity, *refs),
        out_shape=[half, half],
        in_specs=[VMEM],
        out_specs=[VMEM] * 2,
        compiler_params=pltpu.CompilerParams(vmem_limit_bytes=VMEM_LIMIT),
    )(recv)
    grad_full = lax.all_gather(grad_rows, "etp", axis=1, tiled=True)
    held = [jnp.stack([token_rows, exchange(token_rows, 0)])]
    for step in range(1, steps):
        held.append(exchange(held[-1], step))
    gate_weight, up_weight, down_weight = w_gate[0].T, w_up[0].T, w_down[0]
    weights = [gate_weight, up_weight, down_weight]
    hidden_width, width = down_weight.shape
    square = jax.ShapeDtypeStruct((slots, hidden_width), f32)
    pair_shape = (2, slots, local_width)
    cost = pl.CostEstimate(
        flops=6 * slots * hidden_width * width, bytes_accessed=9 << 20, transcendentals=0
    )
    params = pltpu.CompilerParams(vmem_limit_bytes=VMEM_LIMIT)
    operands = held + weights
    shapes = [square, square] + [
        jax.ShapeDtypeStruct(pair_shape, f32 if k < steps - 1 else bf16) for k in range(steps)
    ]
    gate, up, *parts = pl.pallas_call(
        lambda *refs: forward_kernel(steps, *refs),
        out_shape=shapes,
        in_specs=[VMEM] * len(operands),
        out_specs=[VMEM] * len(shapes),
        compiler_params=params,
        cost_estimate=cost,
    )(*operands)
    input_part = pl.pallas_call(
        backward_kernel,
        out_shape=jax.ShapeDtypeStruct((slots, width), bf16),
        in_specs=[ANY] + [VMEM] * 5,
        out_specs=ANY,
        scratch_shapes=[
            pltpu.VMEM((slots, width), bf16),
            pltpu.VMEM((slots, width), bf16),
            pltpu.SemaphoreType.DMA((CHUNKS,)),
            pltpu.SemaphoreType.DMA((CHUNKS,)),
        ],
        compiler_params=params,
        cost_estimate=cost,
    )(grad_full, *weights, gate, up)
    input_local = lax.psum_scatter(input_part, "etp", scatter_dimension=1, tiled=True)
    out_sum = parts[-1]
    for step in reversed(range(1, steps)):
        out_sum = sum_step(parts, out_sum, step)
    unsorted = pl.pallas_call(
        lambda *refs: unsort_kernel(capacity, *refs),
        out_shape=jax.ShapeDtypeStruct((rows, local_width), bf16),
        in_specs=[VMEM] * 3,
        out_specs=VMEM,
        compiler_params=params,
    )(out_sum, exchange(out_sum[1], 0), input_local)
    back = lax.all_to_all(
        unsorted.reshape(owners, 2 * capacity, local_width), "ep", split_axis=0, concat_axis=0, tiled=True
    ).reshape(rows, local_width)
    mine = jax.ShapeDtypeStruct((tok_rows, local_width), bf16)
    mixed, grad_tokens = pl.pallas_call(
        lambda *refs: combine_kernel(capacity, *refs),
        out_shape=[mine, mine],
        in_specs=[VMEM] * 3,
        out_specs=[VMEM] * 2,
        compiler_params=pltpu.CompilerParams(vmem_limit_bytes=VMEM_LIMIT),
    )(routes.T, route_weight.T, back)
    return (mixed, grad_tokens)


def solution(mesh):
    in_specs = (
        P("ep", "etp"),
        P("ep", None),
        P("ep", None),
        P("ep", "etp"),
        P("ep", None, "etp"),
        P("ep", None, "etp"),
        P("ep", "etp", None),
    )
    out_specs = (P("ep", "etp"), P("ep", "etp"))
    return jax.shard_map(
        on_device, mesh=mesh, in_specs=in_specs, out_specs=out_specs, check_vma=False
    )
```

```python
import jax
import jax.numpy as jnp
from jax import lax
from jax.experimental import pallas as pl
from jax.experimental.pallas import tpu as pltpu
from jax.sharding import PartitionSpec as P

bf16 = jnp.bfloat16
f32 = jnp.float32
VMEM = pl.BlockSpec(memory_space=pltpu.VMEM)
VMEM_LIMIT = 24 * 1024 * 1024
SHARES = 2


def dot_last(left, right):
    return lax.dot_general(left, right, (((1,), (1,)), ((), ())), preferred_element_type=f32)


def dot(left, right):
    return lax.dot_general(left, right, (((1,), (0,)), ((), ())), preferred_element_type=f32)


def split3(value):
    high = value.astype(bf16)
    rest = value - high.astype(f32)
    middle = rest.astype(bf16)
    return high, middle, (rest - middle.astype(f32)).astype(bf16)


def dot_first(left, right):
    return lax.dot_general(left, right, (((0,), (0,)), ((), ())), preferred_element_type=f32)


def travel_row(slot, kind, capacity):
    return lax.div(slot, capacity) * (2 * capacity) + kind * capacity + lax.rem(slot, capacity)


def picks(capacity, routes, weight, rows):
    shape = (rows, routes.shape[1])
    row = lax.broadcasted_iota(jnp.int32, shape, 0)
    owner = lax.div(row, 2 * capacity)
    named = jnp.zeros(shape, f32)
    scale = jnp.zeros(shape, f32)
    for k in range(routes.shape[0]):
        hit = routes[k : k + 1, :] == owner
        named = jnp.where(hit, 1.0, named)
        scale = jnp.where(hit, weight[k : k + 1, :], scale)
    square = (shape[1], shape[1])
    before = lax.broadcasted_iota(jnp.int32, square, 0) < lax.broadcasted_iota(jnp.int32, square, 1)
    earlier = dot(named.astype(bf16), before.astype(f32).astype(bf16))
    here = earlier == lax.rem(row, capacity).astype(f32)
    gradient = lax.rem(row, 2 * capacity) >= capacity
    return jnp.where(here, named, 0.0), jnp.where(here, scale, 0.0), gradient


def dispatch_kernel(capacity, routes, weight, tokens, grads, send):
    pick, weighted, gradient = picks(capacity, routes, weight, send.shape[0])
    out = dot(jnp.where(gradient, 0.0, pick).astype(bf16), tokens[...])
    for part in split3(jnp.where(gradient, weighted, 0.0)):
        out = out + dot(part, grads[...])
    send[...] = out.astype(bf16)


def sort_kernel(capacity, recv, *out):
    rows = recv.shape[0]
    count = len(out) // 2
    for kind in (0, 1):
        shape = (rows // 2, rows)
        source = travel_row(lax.broadcasted_iota(jnp.int32, shape, 0), kind, capacity)
        place = (source == lax.broadcasted_iota(jnp.int32, shape, 1)).astype(f32).astype(bf16)
        value = dot(place, recv[...]).astype(bf16)
        size = value.shape[0] // count
        for h in range(count):
            out[kind * count + h][...] = value[h * size : (h + 1) * size]


def unsort_kernel(capacity, *refs):
    unsorted = refs[-1]
    rows = unsorted.shape[0]
    total = None
    for kind in (0, 1):
        shares = []
        for h in range(SHARES):
            held, last = refs[2 * (kind * SHARES + h) : 2 * (kind * SHARES + h) + 2]
            shares.append((held[0].astype(f32) + last[...].astype(f32)).astype(bf16))
        local = jnp.concatenate(shares, axis=0)
        shape = (rows, rows // 2)
        target = travel_row(lax.broadcasted_iota(jnp.int32, shape, 1), kind, capacity)
        place = (target == lax.broadcasted_iota(jnp.int32, shape, 0)).astype(f32).astype(bf16)
        now = dot(place, local)
        total = now if total is None else total + now
    unsorted[...] = total.astype(bf16)


def combine_kernel(capacity, routes, weight, back, mixed, grad_tokens):
    pick, weighted, gradient = picks(capacity, routes, weight, back.shape[0])
    rows = back[...]
    out = None
    for part in split3(jnp.where(gradient, 0.0, weighted)):
        now = dot_first(part, rows)
        out = now if out is None else out + now
    mixed[...] = out.astype(bf16)
    grad_tokens[...] = dot_first(jnp.where(gradient, pick, 0.0).astype(bf16), rows).astype(bf16)


def exchange(value, step, chain):
    size, owners = lax.axis_size("etp"), lax.axis_size("ep")
    pairs = []
    for y in range(size):
        for j in range(owners):
            sign = 1 if (y + j + step + chain) % 2 == 0 else -1
            pairs.append((y * owners + j, (y + sign) % size * owners + j))
    return lax.ppermute(value, ("etp", "ep"), pairs)


def columns_of(steps, width, chain):
    size = 2 * steps
    y = lax.axis_index("etp")
    sign = 1 - 2 * lax.rem(y + lax.axis_index("ep") + chain, 2)
    out = []
    for k in range(steps):
        turn = sign if k % 2 == 0 else -sign
        blocks = [lax.rem(y + turn * (k + b) + 2 * size, size) for b in (0, 1)]
        out.append([pl.ds(pl.multiple_of(block * width, width), width) for block in blocks])
    return out


def split_refs(steps, refs):
    count = steps * SHARES
    held = [refs[k * SHARES : (k + 1) * SHARES] for k in range(steps)]
    last = refs[count + 5 :]
    parts = [last[k * SHARES : (k + 1) * SHARES] for k in range(steps)]
    return held, refs[count : count + 3], refs[count + 3 : count + 5], parts


def rows_of(shares, block):
    return jnp.concatenate([share[block] for share in shares], axis=0)


def store(shares, block, value):
    count = value.shape[0] // SHARES
    for h, share in enumerate(shares):
        share[block] = value[h * count : (h + 1) * count].astype(share.dtype)


def forward_kernel(steps, *refs):
    held, (gate_w, up_w, down_w), (gate_ref, up_ref), parts = split_refs(steps, refs)
    columns = columns_of(steps, held[0][0].shape[2], 0)
    gate = up = None
    for k in range(steps):
        for b in (0, 1):
            rows = rows_of(held[k], b)
            gate_now = dot_last(rows, gate_w[:, columns[k][b]])
            up_now = dot_last(rows, up_w[:, columns[k][b]])
            gate = gate_now if gate is None else gate + gate_now
            up = up_now if up is None else up + up_now
    gate_ref[...] = gate
    up_ref[...] = up
    hidden = (gate * jax.nn.sigmoid(gate) * up).astype(bf16)
    for k in reversed(range(steps)):
        for b in (0, 1):
            store(parts[k], b, dot(hidden, down_w[:, columns[k][b]]))


def backward_kernel(steps, *refs):
    held, (gate_w, up_w, down_w), (gate_ref, up_ref), parts = split_refs(steps, refs)
    columns = columns_of(steps, held[0][0].shape[2], 1)
    hidden_grad = None
    for k in range(steps):
        for b in (0, 1):
            now = dot_last(rows_of(held[k], b), down_w[:, columns[k][b]])
            hidden_grad = now if hidden_grad is None else hidden_grad + now
    gate, up = gate_ref[...], up_ref[...]
    squash = jax.nn.sigmoid(gate)
    up_grad = (hidden_grad * (gate * squash)).astype(bf16)
    gate_grad = (hidden_grad * up * squash * (1.0 + gate * (1.0 - squash))).astype(bf16)
    for k in reversed(range(steps)):
        for b in (0, 1):
            part = dot(gate_grad, gate_w[:, columns[k][b]]) + dot(up_grad, up_w[:, columns[k][b]])
            store(parts[k], b, part)


def call(kernel, steps, operands, extra_shapes, pair_shape, flops):
    shapes = extra_shapes + [
        jax.ShapeDtypeStruct(pair_shape, f32 if k < steps - 1 else bf16)
        for k in range(steps)
        for _ in range(SHARES)
    ]
    return pl.pallas_call(
        lambda *refs: kernel(steps, *refs),
        out_shape=shapes,
        in_specs=[VMEM] * len(operands),
        out_specs=[VMEM] * len(shapes),
        compiler_params=pltpu.CompilerParams(vmem_limit_bytes=VMEM_LIMIT),
        cost_estimate=pl.CostEstimate(flops=flops, bytes_accessed=9 << 20, transcendentals=0),
    )(*operands)


def sum_step(part, arrived, step, chain):
    return (part + exchange(arrived, step, chain).astype(f32)).astype(bf16)


def on_device(tokens, routes, route_weight, grad_out, w_gate, w_up, w_down):
    owners, steps = lax.axis_size("ep"), lax.axis_size("etp") // 2
    tok_rows, local_width = tokens.shape
    top_count = routes.shape[1]
    capacity = min(tok_rows, max(2, (3 * tok_rows * top_count + 2 * owners - 1) // (2 * owners)))
    slots = owners * capacity
    rows = 2 * slots
    send = pl.pallas_call(
        lambda *refs: dispatch_kernel(capacity, *refs),
        out_shape=jax.ShapeDtypeStruct((rows, local_width), bf16),
        compiler_params=pltpu.CompilerParams(vmem_limit_bytes=VMEM_LIMIT),
    )(routes.T, route_weight.T, tokens, grad_out)
    recv = lax.all_to_all(
        send.reshape(owners, 2 * capacity, local_width), "ep", split_axis=0, concat_axis=0, tiled=True
    ).reshape(rows, local_width)
    share = jax.ShapeDtypeStruct((slots // SHARES, local_width), bf16)
    own = pl.pallas_call(
        lambda *refs: sort_kernel(capacity, *refs),
        out_shape=[share] * (2 * SHARES),
        in_specs=[VMEM],
        out_specs=[VMEM] * (2 * SHARES),
        compiler_params=pltpu.CompilerParams(vmem_limit_bytes=VMEM_LIMIT),
    )(recv)
    kinds = [q // SHARES for q in range(2 * SHARES)]
    arrived = lax.optimization_barrier([exchange(own[q], 0, kinds[q]) for q in range(2 * SHARES)])
    held = [[jnp.stack([own[q], arrived[q]])] for q in range(2 * SHARES)]
    for step in range(1, steps):
        for q in range(2 * SHARES):
            held[q].append(exchange(held[q][-1], step, kinds[q]))
    token_held, grad_held = (
        [held[kind * SHARES + h][k] for k in range(steps) for h in range(SHARES)] for kind in (0, 1)
    )
    gate_weight, up_weight, down_weight = w_gate[0].T, w_up[0].T, w_down[0]
    weights = [gate_weight, up_weight, down_weight]
    hidden_width, width = down_weight.shape
    square = jax.ShapeDtypeStruct((slots, hidden_width), f32)
    pair_shape = (2, slots // SHARES, local_width)
    flops = 2 * slots * hidden_width * width
    gate, up, *out_parts = call(
        forward_kernel, steps, token_held + weights, [square, square], pair_shape, 3 * flops
    )
    input_parts = call(
        backward_kernel, steps, grad_held + weights + [gate, up], [], pair_shape, 3 * flops
    )
    parts = [
        [(out_parts, input_parts)[kind][k * SHARES + h] for k in range(steps)]
        for kind in (0, 1)
        for h in range(SHARES)
    ]
    sums = [parts[q][-1] for q in range(2 * SHARES)]
    for step in reversed(range(1, steps)):
        sums = [sum_step(parts[q][step - 1], sums[q], step, kinds[q]) for q in range(2 * SHARES)]
    ends = [ref for q in range(2 * SHARES) for ref in (sums[q], exchange(sums[q][1], 0, kinds[q]))]
    unsorted = pl.pallas_call(
        lambda *refs: unsort_kernel(capacity, *refs),
        out_shape=jax.ShapeDtypeStruct((rows, local_width), bf16),
        in_specs=[VMEM] * len(ends),
        out_specs=VMEM,
        compiler_params=pltpu.CompilerParams(vmem_limit_bytes=VMEM_LIMIT),
    )(*ends)
    back = lax.all_to_all(
        unsorted.reshape(owners, 2 * capacity, local_width), "ep", split_axis=0, concat_axis=0, tiled=True
    ).reshape(rows, local_width)
    mine = jax.ShapeDtypeStruct((tok_rows, local_width), bf16)
    mixed, grad_tokens = pl.pallas_call(
        lambda *refs: combine_kernel(capacity, *refs),
        out_shape=[mine, mine],
        in_specs=[VMEM] * 3,
        out_specs=[VMEM] * 2,
        compiler_params=pltpu.CompilerParams(vmem_limit_bytes=VMEM_LIMIT),
    )(routes.T, route_weight.T, back)
    return (mixed, grad_tokens)


def solution(mesh):
    in_specs = (
        P("ep", "etp"),
        P("ep", None),
        P("ep", None),
        P("ep", "etp"),
        P("ep", None, "etp"),
        P("ep", None, "etp"),
        P("ep", "etp", None),
    )
    out_specs = (P("ep", "etp"), P("ep", "etp"))
    return jax.shard_map(
        on_device, mesh=mesh, in_specs=in_specs, out_specs=out_specs, check_vma=False
    )
```

```python
import jax
import jax.numpy as jnp
from jax import lax
from jax.experimental import pallas as pl
from jax.experimental.pallas import tpu as pltpu
from jax.sharding import PartitionSpec as P

bf16 = jnp.bfloat16
f32 = jnp.float32
VMEM = pl.BlockSpec(memory_space=pltpu.VMEM)
HBM = pl.BlockSpec(memory_space=pltpu.HBM)
VMEM_LIMIT = 16 * 1024 * 1024
BIG = 60 * 1024 * 1024


def dot_last(left, right):
    return lax.dot_general(left, right, (((1,), (1,)), ((), ())), preferred_element_type=f32)


def dot(left, right):
    return lax.dot_general(left, right, (((1,), (0,)), ((), ())), preferred_element_type=f32)


def split3(value):
    high = value.astype(bf16)
    rest = value - high.astype(f32)
    middle = rest.astype(bf16)
    return high, middle, (rest - middle.astype(f32)).astype(bf16)


def dot_first(left, right):
    return lax.dot_general(left, right, (((0,), (0,)), ((), ())), preferred_element_type=f32)


def travel_row(slot, kind, capacity):
    return lax.div(slot, capacity) * (2 * capacity) + kind * capacity + lax.rem(slot, capacity)


def picks(capacity, routes, weight, rows):
    shape = (rows, routes.shape[1])
    row = lax.broadcasted_iota(jnp.int32, shape, 0)
    owner = lax.div(row, 2 * capacity)
    named = jnp.zeros(shape, f32)
    scale = jnp.zeros(shape, f32)
    for k in range(routes.shape[0]):
        hit = routes[k : k + 1, :] == owner
        named = jnp.where(hit, 1.0, named)
        scale = jnp.where(hit, weight[k : k + 1, :], scale)
    square = (shape[1], shape[1])
    before = lax.broadcasted_iota(jnp.int32, square, 0) < lax.broadcasted_iota(jnp.int32, square, 1)
    earlier = dot(named.astype(bf16), before.astype(f32).astype(bf16))
    here = earlier == lax.rem(row, capacity).astype(f32)
    gradient = lax.rem(row, 2 * capacity) >= capacity
    return jnp.where(here, named, 0.0), jnp.where(here, scale, 0.0), gradient


def dispatch_kernel(capacity, *refs):
    outside, send, inside, sems = refs[:4], refs[4], refs[5:9], refs[9]
    copies = [pltpu.make_async_copy(outside[i], inside[i], sems.at[i]) for i in range(4)]
    for copy in copies:
        copy.start()
    for copy in copies:
        copy.wait()
    routes, weight, tokens, grads = inside
    pick, weighted, gradient = picks(capacity, routes, weight, send.shape[0])
    out = dot(jnp.where(gradient, 0.0, pick).astype(bf16), tokens[...])
    for part in split3(jnp.where(gradient, weighted, 0.0)):
        out = out + dot(part, grads[...])
    send[...] = out.astype(bf16)


def sort_kernel(capacity, recv, down_w, token_rows, grad_rows):
    del down_w
    rows = recv.shape[0]
    for kind, out in ((0, token_rows), (1, grad_rows)):
        shape = (rows // 2, rows)
        source = travel_row(lax.broadcasted_iota(jnp.int32, shape, 0), kind, capacity)
        place = (source == lax.broadcasted_iota(jnp.int32, shape, 1)).astype(f32).astype(bf16)
        out[...] = dot(place, recv[...]).astype(bf16)


def unsort_kernel(capacity, out_sum, out_last, input_sum, input_last, unsorted):
    rows = unsorted.shape[0]
    total = None
    for kind, held, last in ((0, out_sum, out_last), (1, input_sum, input_last)):
        local = (held[0].astype(f32) + last[...].astype(f32)).astype(bf16)
        shape = (rows, rows // 2)
        target = travel_row(lax.broadcasted_iota(jnp.int32, shape, 1), kind, capacity)
        place = (target == lax.broadcasted_iota(jnp.int32, shape, 0)).astype(f32).astype(bf16)
        now = dot(place, local)
        total = now if total is None else total + now
    unsorted[...] = total.astype(bf16)


def combine_kernel(capacity, routes, weight, back, mixed, grad_tokens):
    pick, weighted, gradient = picks(capacity, routes, weight, back.shape[0])
    rows = back[...]
    out = None
    for part in split3(jnp.where(gradient, 0.0, weighted)):
        now = dot_first(part, rows)
        out = now if out is None else out + now
    mixed[...] = out.astype(bf16)
    grad_tokens[...] = dot_first(jnp.where(gradient, pick, 0.0).astype(bf16), rows).astype(bf16)


def exchange(value, step, chain):
    size, owners = lax.axis_size("etp"), lax.axis_size("ep")
    pairs = []
    for y in range(size):
        for j in range(owners):
            sign = 1 if (y + j + step + chain) % 2 == 0 else -1
            pairs.append((y * owners + j, (y + sign) % size * owners + j))
    return lax.ppermute(value, ("etp", "ep"), pairs)


def columns_of(steps, width, chain):
    size = 2 * steps
    y = lax.axis_index("etp")
    sign = 1 - 2 * lax.rem(y + lax.axis_index("ep") + chain, 2)
    out = []
    for k in range(steps):
        turn = sign if k % 2 == 0 else -sign
        blocks = [lax.rem(y + turn * (k + b) + 2 * size, size) for b in (0, 1)]
        out.append([pl.ds(pl.multiple_of(block * width, width), width) for block in blocks])
    return out


def forward_kernel(steps, *refs):
    held, (gate_w, up_w, down_w) = refs[:steps], refs[steps : steps + 3]
    gate_ref, up_ref = refs[steps + 3 : steps + 5]
    parts = refs[steps + 5 :]
    columns = columns_of(steps, held[0].shape[2], 0)
    gate = up = None
    for k in range(steps):
        for b in (0, 1):
            rows = held[k][b]
            gate_now = dot_last(rows, gate_w[:, columns[k][b]])
            up_now = dot_last(rows, up_w[:, columns[k][b]])
            gate = gate_now if gate is None else gate + gate_now
            up = up_now if up is None else up + up_now
    gate_ref[...] = gate
    up_ref[...] = up
    hidden = (gate * jax.nn.sigmoid(gate) * up).astype(bf16)
    for k in reversed(range(steps)):
        for b in (0, 1):
            parts[k][b] = dot(hidden, down_w[:, columns[k][b]]).astype(parts[k].dtype)


def backward_kernel(steps, *refs):
    held, (gate_w, up_w, down_w) = refs[:steps], refs[steps : steps + 3]
    gate_ref, up_ref = refs[steps + 3 : steps + 5]
    parts = refs[steps + 5 :]
    columns = columns_of(steps, held[0].shape[2], 1)
    hidden_grad = None
    for k in range(steps):
        for b in (0, 1):
            now = dot_last(held[k][b], down_w[:, columns[k][b]])
            hidden_grad = now if hidden_grad is None else hidden_grad + now
    gate, up = gate_ref[...], up_ref[...]
    squash = jax.nn.sigmoid(gate)
    up_grad = (hidden_grad * (gate * squash)).astype(bf16)
    gate_grad = (hidden_grad * up * squash * (1.0 + gate * (1.0 - squash))).astype(bf16)
    for k in reversed(range(steps)):
        for b in (0, 1):
            part = dot(gate_grad, gate_w[:, columns[k][b]]) + dot(up_grad, up_w[:, columns[k][b]])
            parts[k][b] = part.astype(parts[k].dtype)


def call(kernel, steps, operands, extra_shapes, pair_shape, flops):
    shapes = extra_shapes + [
        jax.ShapeDtypeStruct(pair_shape, f32 if k < steps - 1 else bf16) for k in range(steps)
    ]
    return pl.pallas_call(
        lambda *refs: kernel(steps, *refs),
        out_shape=shapes,
        in_specs=[VMEM] * len(operands),
        out_specs=[VMEM] * len(shapes),
        compiler_params=pltpu.CompilerParams(vmem_limit_bytes=VMEM_LIMIT),
        cost_estimate=pl.CostEstimate(flops=flops, bytes_accessed=9 << 20, transcendentals=0),
    )(*operands)


def sum_step(parts, arrived, step, chain):
    received = exchange(arrived, step, chain)
    return (parts[step - 1] + received.astype(f32)).astype(bf16)


def on_device(tokens, routes, route_weight, grad_out, w_gate, w_up, w_down):
    owners, steps = lax.axis_size("ep"), lax.axis_size("etp") // 2
    tok_rows, local_width = tokens.shape
    top_count = routes.shape[1]
    capacity = min(tok_rows, max(2, (3 * tok_rows * top_count + 2 * owners - 1) // (2 * owners)))
    slots = owners * capacity
    rows = 2 * slots
    inputs = (routes.T, route_weight.T, tokens, grad_out)
    send = pl.pallas_call(
        lambda *refs: dispatch_kernel(capacity, *refs),
        out_shape=jax.ShapeDtypeStruct((rows, local_width), bf16),
        in_specs=[HBM] * 4,
        out_specs=VMEM,
        scratch_shapes=[pltpu.VMEM(value.shape, value.dtype) for value in inputs]
        + [pltpu.SemaphoreType.DMA((4,))],
        compiler_params=pltpu.CompilerParams(vmem_limit_bytes=BIG),
    )(*inputs)
    recv = lax.all_to_all(
        send.reshape(owners, 2 * capacity, local_width), "ep", split_axis=0, concat_axis=0, tiled=True
    ).reshape(rows, local_width)
    half = jax.ShapeDtypeStruct((slots, local_width), bf16)
    token_rows, grad_rows = pl.pallas_call(
        lambda *refs: sort_kernel(capacity, *refs),
        out_shape=[half, half],
        in_specs=[VMEM, VMEM],
        out_specs=[VMEM] * 2,
        compiler_params=pltpu.CompilerParams(vmem_limit_bytes=VMEM_LIMIT),
    )(recv, w_down[0])
    token_next, grad_next = lax.optimization_barrier(
        (exchange(token_rows, 0, 0), exchange(grad_rows, 0, 1))
    )
    token_held = [jnp.stack([token_rows, token_next])]
    grad_held = [jnp.stack([grad_rows, grad_next])]
    for step in range(1, steps):
        token_held.append(exchange(token_held[-1], step, 0))
        grad_held.append(exchange(grad_held[-1], step, 1))
    gate_weight, up_weight, down_weight = w_gate[0].T, w_up[0].T, w_down[0]
    weights = [gate_weight, up_weight, down_weight]
    hidden_width, width = down_weight.shape
    square = jax.ShapeDtypeStruct((slots, hidden_width), f32)
    pair_shape = (2, slots, local_width)
    flops = 2 * slots * hidden_width * width
    gate, up, *out_parts = call(
        forward_kernel, steps, token_held + weights, [square, square], pair_shape, 3 * flops
    )
    input_parts = call(
        backward_kernel, steps, grad_held + weights + [gate, up], [], pair_shape, 3 * flops
    )
    out_sum, input_sum = out_parts[-1], input_parts[-1]
    for step in reversed(range(1, steps)):
        out_sum = sum_step(out_parts, out_sum, step, 0)
        input_sum = sum_step(input_parts, input_sum, step, 1)
    unsorted = pl.pallas_call(
        lambda *refs: unsort_kernel(capacity, *refs),
        out_shape=jax.ShapeDtypeStruct((rows, local_width), bf16),
        in_specs=[VMEM] * 4,
        out_specs=VMEM,
        compiler_params=pltpu.CompilerParams(vmem_limit_bytes=VMEM_LIMIT),
    )(out_sum, exchange(out_sum[1], 0, 0), input_sum, exchange(input_sum[1], 0, 1))
    back = lax.all_to_all(
        unsorted.reshape(owners, 2 * capacity, local_width), "ep", split_axis=0, concat_axis=0, tiled=True
    ).reshape(rows, local_width)
    mine = jax.ShapeDtypeStruct((tok_rows, local_width), bf16)
    mixed, grad_tokens = pl.pallas_call(
        lambda *refs: combine_kernel(capacity, *refs),
        out_shape=[mine, mine],
        in_specs=[VMEM] * 3,
        out_specs=[VMEM] * 2,
        compiler_params=pltpu.CompilerParams(vmem_limit_bytes=VMEM_LIMIT),
    )(routes.T, route_weight.T, back)
    return (mixed, grad_tokens)


def solution(mesh):
    in_specs = (
        P("ep", "etp"),
        P("ep", None),
        P("ep", None),
        P("ep", "etp"),
        P("ep", None, "etp"),
        P("ep", None, "etp"),
        P("ep", "etp", None),
    )
    out_specs = (P("ep", "etp"), P("ep", "etp"))
    return jax.shard_map(
        on_device, mesh=mesh, in_specs=in_specs, out_specs=out_specs, check_vma=False
    )
```

```python
import jax
import jax.numpy as jnp
from jax import lax
from jax.experimental import pallas as pl
from jax.experimental.pallas import tpu as pltpu
from jax.sharding import PartitionSpec as P

bf16 = jnp.bfloat16
f32 = jnp.float32
VMEM = pl.BlockSpec(memory_space=pltpu.VMEM)
HBM = pl.BlockSpec(memory_space=pltpu.HBM)
VMEM_LIMIT = 16 * 1024 * 1024
BIG = 60 * 1024 * 1024


def dot_last(left, right):
    return lax.dot_general(left, right, (((1,), (1,)), ((), ())), preferred_element_type=f32)


def dot(left, right):
    return lax.dot_general(left, right, (((1,), (0,)), ((), ())), preferred_element_type=f32)


def split3(value):
    high = value.astype(bf16)
    rest = value - high.astype(f32)
    middle = rest.astype(bf16)
    return high, middle, (rest - middle.astype(f32)).astype(bf16)


def dot_first(left, right):
    return lax.dot_general(left, right, (((0,), (0,)), ((), ())), preferred_element_type=f32)


def travel_row(slot, kind, capacity):
    return lax.div(slot, capacity) * (2 * capacity) + kind * capacity + lax.rem(slot, capacity)


def picks(capacity, routes, weight, rows):
    shape = (rows, routes.shape[1])
    row = lax.broadcasted_iota(jnp.int32, shape, 0)
    owner = lax.div(row, 2 * capacity)
    named = jnp.zeros(shape, f32)
    scale = jnp.zeros(shape, f32)
    for k in range(routes.shape[0]):
        hit = routes[k : k + 1, :] == owner
        named = jnp.where(hit, 1.0, named)
        scale = jnp.where(hit, weight[k : k + 1, :], scale)
    square = (shape[1], shape[1])
    before = lax.broadcasted_iota(jnp.int32, square, 0) < lax.broadcasted_iota(jnp.int32, square, 1)
    earlier = dot(named.astype(bf16), before.astype(f32).astype(bf16))
    here = earlier == lax.rem(row, capacity).astype(f32)
    gradient = lax.rem(row, 2 * capacity) >= capacity
    return jnp.where(here, named, 0.0), jnp.where(here, scale, 0.0), gradient


def dispatch_kernel(capacity, *refs):
    outside, send, inside, sems = refs[:4], refs[4], refs[5:9], refs[9]
    copies = [pltpu.make_async_copy(outside[i], inside[i], sems.at[i]) for i in range(4)]
    for copy in copies:
        copy.start()
    for copy in copies:
        copy.wait()
    routes, weight, tokens, grads = inside
    pick, weighted, gradient = picks(capacity, routes, weight, send.shape[0])
    out = dot(jnp.where(gradient, 0.0, pick).astype(bf16), tokens[...])
    for part in split3(jnp.where(gradient, weighted, 0.0)):
        out = out + dot(part, grads[...])
    send[...] = out.astype(bf16)


def sort_kernel(capacity, recv, down_w, out):
    del down_w
    rows = recv.shape[0]
    for kind in (0, 1):
        shape = (rows // 2, rows)
        source = travel_row(lax.broadcasted_iota(jnp.int32, shape, 0), kind, capacity)
        place = (source == lax.broadcasted_iota(jnp.int32, shape, 1)).astype(f32).astype(bf16)
        out[kind * (rows // 2) : (kind + 1) * (rows // 2)] = dot(place, recv[...]).astype(bf16)


def unsort_kernel(capacity, held, last, unsorted):
    rows = unsorted.shape[0]
    half = rows // 2
    total = None
    for kind in (0, 1):
        part = slice(kind * half, (kind + 1) * half)
        local = (held[0, part].astype(f32) + last[part].astype(f32)).astype(bf16)
        target = travel_row(lax.broadcasted_iota(jnp.int32, (rows, half), 1), kind, capacity)
        place = (target == lax.broadcasted_iota(jnp.int32, (rows, half), 0)).astype(f32).astype(bf16)
        now = dot(place, local)
        total = now if total is None else total + now
    unsorted[...] = total.astype(bf16)


def combine_kernel(capacity, routes, weight, back, mixed, grad_tokens):
    pick, weighted, gradient = picks(capacity, routes, weight, back.shape[0])
    rows = back[...]
    out = None
    for part in split3(jnp.where(gradient, 0.0, weighted)):
        now = dot_first(part, rows)
        out = now if out is None else out + now
    mixed[...] = out.astype(bf16)
    grad_tokens[...] = dot_first(jnp.where(gradient, pick, 0.0).astype(bf16), rows).astype(bf16)


def exchange(value, step):
    size, owners = lax.axis_size("etp"), lax.axis_size("ep")
    pairs = []
    for y in range(size):
        for j in range(owners):
            sign = 1 if (y + j + step) % 2 == 0 else -1
            pairs.append((y * owners + j, (y + sign) % size * owners + j))
    return lax.ppermute(value, ("etp", "ep"), pairs)


def columns_of(steps, width):
    size = 2 * steps
    y = lax.axis_index("etp")
    sign = 1 - 2 * lax.rem(y + lax.axis_index("ep"), 2)
    out = []
    for k in range(steps):
        turn = sign if k % 2 == 0 else -sign
        blocks = [lax.rem(y + turn * (k + b) + 2 * size, size) for b in (0, 1)]
        out.append([pl.ds(pl.multiple_of(block * width, width), width) for block in blocks])
    return out


def add_pair(held, columns, weights, totals):
    slots = held.shape[1] // 2
    gate_w, up_w, down_w = weights
    for b in (0, 1):
        token_rows, grad_rows = held[b, :slots], held[b, slots:]
        now = (
            dot_last(token_rows, gate_w[:, columns[b]]),
            dot_last(token_rows, up_w[:, columns[b]]),
            dot_last(grad_rows, down_w[:, columns[b]]),
        )
        totals = now if totals is None else tuple(x + y for x, y in zip(totals, now))
    return totals


def store_pair(part, columns, weights, hidden, gate_grad, up_grad):
    slots = part.shape[1] // 2
    gate_w, up_w, down_w = weights
    for b in (0, 1):
        part[b, :slots] = dot(hidden, down_w[:, columns[b]]).astype(part.dtype)
        now = dot(gate_grad, gate_w[:, columns[b]]) + dot(up_grad, up_w[:, columns[b]])
        part[b, slots:] = now.astype(part.dtype)


def first_kernel(steps, *refs):
    held, weights, totals = refs[: steps - 1], refs[steps - 1 : steps + 2], refs[steps + 2 :]
    columns = columns_of(steps, held[0].shape[2])
    sums = None
    for k in range(steps - 1):
        sums = add_pair(held[k], columns[k], weights, sums)
    for total, value in zip(totals, sums):
        total[...] = value


def middle_kernel(steps, *refs):
    held, weights, totals = refs[0], refs[1:4], refs[4:7]
    hidden_ref, gate_grad_ref, up_grad_ref, part = refs[7:]
    columns = columns_of(steps, held.shape[2])[-1]
    gate, up, hidden_grad = add_pair(held, columns, weights, tuple(x[...] for x in totals))
    squash = jax.nn.sigmoid(gate)
    active = gate * squash
    hidden = (active * up).astype(bf16)
    up_grad = (hidden_grad * active).astype(bf16)
    gate_grad = (hidden_grad * up * squash * (1.0 + gate * (1.0 - squash))).astype(bf16)
    hidden_ref[...] = hidden
    gate_grad_ref[...] = gate_grad
    up_grad_ref[...] = up_grad
    store_pair(part, columns, weights, hidden, gate_grad, up_grad)


def last_kernel(steps, *refs):
    weights, (hidden, gate_grad, up_grad), parts = refs[:3], refs[3:6], refs[6:]
    columns = columns_of(steps, parts[0].shape[2])
    for k in reversed(range(steps - 1)):
        store_pair(parts[k], columns[k], weights, hidden[...], gate_grad[...], up_grad[...])


def call(kernel, steps, operands, shapes, flops):
    return pl.pallas_call(
        lambda *refs: kernel(steps, *refs),
        out_shape=shapes,
        in_specs=[VMEM] * len(operands),
        out_specs=[VMEM] * len(shapes),
        compiler_params=pltpu.CompilerParams(vmem_limit_bytes=VMEM_LIMIT),
        cost_estimate=pl.CostEstimate(flops=flops, bytes_accessed=6 << 20, transcendentals=0),
    )(*operands)


def sum_step(part, arrived, step):
    return (part + exchange(arrived, step).astype(f32)).astype(bf16)


def on_device(tokens, routes, route_weight, grad_out, w_gate, w_up, w_down):
    owners, steps = lax.axis_size("ep"), lax.axis_size("etp") // 2
    tok_rows, local_width = tokens.shape
    top_count = routes.shape[1]
    capacity = min(tok_rows, max(2, (3 * tok_rows * top_count + 2 * owners - 1) // (2 * owners)))
    slots = owners * capacity
    rows = 2 * slots
    inputs = (routes.T, route_weight.T, tokens, grad_out)
    send = pl.pallas_call(
        lambda *refs: dispatch_kernel(capacity, *refs),
        out_shape=jax.ShapeDtypeStruct((rows, local_width), bf16),
        in_specs=[HBM] * 4,
        out_specs=VMEM,
        scratch_shapes=[pltpu.VMEM(value.shape, value.dtype) for value in inputs]
        + [pltpu.SemaphoreType.DMA((4,))],
        compiler_params=pltpu.CompilerParams(vmem_limit_bytes=BIG),
    )(*inputs)
    recv = lax.all_to_all(
        send.reshape(owners, 2 * capacity, local_width), "ep", split_axis=0, concat_axis=0, tiled=True
    ).reshape(rows, local_width)
    own = pl.pallas_call(
        lambda *refs: sort_kernel(capacity, *refs),
        out_shape=jax.ShapeDtypeStruct((rows, local_width), bf16),
        in_specs=[VMEM] * 2,
        out_specs=VMEM,
        compiler_params=pltpu.CompilerParams(vmem_limit_bytes=VMEM_LIMIT),
    )(recv, w_down[0])
    held = [jnp.stack([own, exchange(own, 0)])]
    for step in range(1, steps):
        held.append(exchange(held[-1], step))
    weights = [w_gate[0].T, w_up[0].T, w_down[0]]
    hidden_width, width = weights[2].shape
    square = jax.ShapeDtypeStruct((slots, hidden_width), f32)
    factor = jax.ShapeDtypeStruct((slots, hidden_width), bf16)
    pair = (2, rows, local_width)
    flops = 6 * slots * hidden_width * width // steps
    totals = call(first_kernel, steps, held[:-1] + weights, [square] * 3, flops * (steps - 1))
    *factors, total = call(
        middle_kernel,
        steps,
        [held[-1]] + weights + list(totals),
        [factor] * 3 + [jax.ShapeDtypeStruct(pair, bf16)],
        flops * 2,
    )
    parts = call(
        last_kernel,
        steps,
        weights + factors,
        [jax.ShapeDtypeStruct(pair, f32)] * (steps - 1),
        flops * (steps - 1),
    )
    for step in reversed(range(1, steps)):
        total = sum_step(parts[step - 1], total, step)
    unsorted = pl.pallas_call(
        lambda *refs: unsort_kernel(capacity, *refs),
        out_shape=jax.ShapeDtypeStruct((rows, local_width), bf16),
        in_specs=[VMEM] * 2,
        out_specs=VMEM,
        compiler_params=pltpu.CompilerParams(vmem_limit_bytes=VMEM_LIMIT),
    )(total, exchange(total[1], 0))
    back = lax.all_to_all(
        unsorted.reshape(owners, 2 * capacity, local_width), "ep", split_axis=0, concat_axis=0, tiled=True
    ).reshape(rows, local_width)
    mine = jax.ShapeDtypeStruct((tok_rows, local_width), bf16)
    mixed, grad_tokens = pl.pallas_call(
        lambda *refs: combine_kernel(capacity, *refs),
        out_shape=[mine, mine],
        in_specs=[VMEM] * 3,
        out_specs=[VMEM] * 2,
        compiler_params=pltpu.CompilerParams(vmem_limit_bytes=VMEM_LIMIT),
    )(routes.T, route_weight.T, back)
    return (mixed, grad_tokens)


def solution(mesh):
    in_specs = (
        P("ep", "etp"),
        P("ep", None),
        P("ep", None),
        P("ep", "etp"),
        P("ep", None, "etp"),
        P("ep", None, "etp"),
        P("ep", "etp", None),
    )
    out_specs = (P("ep", "etp"), P("ep", "etp"))
    return jax.shard_map(
        on_device, mesh=mesh, in_specs=in_specs, out_specs=out_specs, check_vma=False
    )
```

```python
import functools

import jax
import jax.numpy as jnp
from jax import lax
from jax.experimental import pallas as pl
from jax.experimental.pallas import tpu as pltpu
from jax.sharding import PartitionSpec as P

bf16 = jnp.bfloat16
f32 = jnp.float32
VMEM = pl.BlockSpec(memory_space=pltpu.VMEM)
HBM = pl.BlockSpec(memory_space=pltpu.HBM)
VMEM_LIMIT = 16 * 1024 * 1024
BIG = 60 * 1024 * 1024


def dot_last(left, right):
    return lax.dot_general(left, right, (((1,), (1,)), ((), ())), preferred_element_type=f32)


def dot(left, right):
    return lax.dot_general(left, right, (((1,), (0,)), ((), ())), preferred_element_type=f32)


def split3(value):
    high = value.astype(bf16)
    rest = value - high.astype(f32)
    middle = rest.astype(bf16)
    return high, middle, (rest - middle.astype(f32)).astype(bf16)


def dot_first(left, right):
    return lax.dot_general(left, right, (((0,), (0,)), ((), ())), preferred_element_type=f32)


def travel_row(slot, kind, capacity):
    return lax.div(slot, capacity) * (2 * capacity) + kind * capacity + lax.rem(slot, capacity)


def picks(capacity, routes, weight, rows):
    shape = (rows, routes.shape[1])
    row = lax.broadcasted_iota(jnp.int32, shape, 0)
    owner = lax.div(row, 2 * capacity)
    named = jnp.zeros(shape, f32)
    scale = jnp.zeros(shape, f32)
    for k in range(routes.shape[0]):
        hit = routes[k : k + 1, :] == owner
        named = jnp.where(hit, 1.0, named)
        scale = jnp.where(hit, weight[k : k + 1, :], scale)
    square = (shape[1], shape[1])
    before = lax.broadcasted_iota(jnp.int32, square, 0) < lax.broadcasted_iota(jnp.int32, square, 1)
    earlier = dot(named.astype(bf16), before.astype(f32).astype(bf16))
    here = earlier == lax.rem(row, capacity).astype(f32)
    gradient = lax.rem(row, 2 * capacity) >= capacity
    return jnp.where(here, named, 0.0), jnp.where(here, scale, 0.0), gradient


def dispatch_kernel(capacity, *refs):
    outside, send, inside, sems = refs[:4], refs[4], refs[5:9], refs[9]
    copies = [pltpu.make_async_copy(outside[i], inside[i], sems.at[i]) for i in range(4)]
    for copy in copies:
        copy.start()
    for copy in copies:
        copy.wait()
    routes, weight, tokens, grads = inside
    pick, weighted, gradient = picks(capacity, routes, weight, send.shape[0])
    out = dot(jnp.where(gradient, 0.0, pick).astype(bf16), tokens[...])
    for part in split3(jnp.where(gradient, weighted, 0.0)):
        out = out + dot(part, grads[...])
    send[...] = out.astype(bf16)


def sort_kernel(capacity, recv, down_w, token_rows, grad_rows):
    del down_w
    rows = recv.shape[0]
    for kind, out in ((0, token_rows), (1, grad_rows)):
        shape = (rows // 2, rows)
        source = travel_row(lax.broadcasted_iota(jnp.int32, shape, 0), kind, capacity)
        place = (source == lax.broadcasted_iota(jnp.int32, shape, 1)).astype(f32).astype(bf16)
        out[...] = dot(place, recv[...]).astype(bf16)


def unsort_kernel(capacity, out_sum, out_last, input_sum, input_last, unsorted):
    rows = unsorted.shape[0]
    total = None
    for kind, held, last in ((0, out_sum, out_last), (1, input_sum, input_last)):
        local = (held[0].astype(f32) + last[...].astype(f32)).astype(bf16)
        shape = (rows, rows // 2)
        target = travel_row(lax.broadcasted_iota(jnp.int32, shape, 1), kind, capacity)
        place = (target == lax.broadcasted_iota(jnp.int32, shape, 0)).astype(f32).astype(bf16)
        now = dot(place, local)
        total = now if total is None else total + now
    unsorted[...] = total.astype(bf16)


def combine_kernel(capacity, routes, weight, back, mixed, grad_tokens):
    pick, weighted, gradient = picks(capacity, routes, weight, back.shape[0])
    rows = back[...]
    out = None
    for part in split3(jnp.where(gradient, 0.0, weighted)):
        now = dot_first(part, rows)
        out = now if out is None else out + now
    mixed[...] = out.astype(bf16)
    grad_tokens[...] = dot_first(jnp.where(gradient, pick, 0.0).astype(bf16), rows).astype(bf16)


def exchange(value, step, chain):
    size, owners = lax.axis_size("etp"), lax.axis_size("ep")
    pairs = []
    for y in range(size):
        for j in range(owners):
            sign = 1 if (y + j + step + chain) % 2 == 0 else -1
            pairs.append((y * owners + j, (y + sign) % size * owners + j))
    return lax.ppermute(value, ("etp", "ep"), pairs)


def columns_of(steps, width, chain):
    size = 2 * steps
    y = lax.axis_index("etp")
    sign = 1 - 2 * lax.rem(y + lax.axis_index("ep") + chain, 2)
    out = []
    for k in range(steps):
        turn = sign if k % 2 == 0 else -sign
        blocks = [lax.rem(y + turn * (k + b) + 2 * size, size) for b in (0, 1)]
        out.append([pl.ds(pl.multiple_of(block * width, width), width) for block in blocks])
    return out


def add_pair(held, columns, weights, totals):
    for b in (0, 1):
        now = [dot_last(held[b], weight[:, columns[b]]) for weight in weights]
        totals = now if totals is None else [x + y for x, y in zip(totals, now)]
    return totals


def store_pair(part, columns, weights, factors):
    for b in (0, 1):
        terms = [dot(f, weight[:, columns[b]]) for f, weight in zip(factors, weights)]
        part[b] = sum(terms[1:], terms[0]).astype(part.dtype)


def early_kernel(steps, chain, *refs):
    held, rest = refs[: steps - 1], refs[steps - 1 :]
    weights, totals = rest[: len(rest) // 2], rest[len(rest) // 2 :]
    columns = columns_of(steps, held[0].shape[2], chain)
    sums = None
    for k in range(steps - 1):
        sums = add_pair(held[k], columns[k], weights, sums)
    for total, value in zip(totals, sums):
        total[...] = value


def forward_kernel(steps, held, gate_w, up_w, down_w, gate_sum, up_sum, gate_ref, up_ref, *parts):
    columns = columns_of(steps, held.shape[2], 0)
    gate, up = add_pair(held, columns[-1], (gate_w, up_w), [gate_sum[...], up_sum[...]])
    gate_ref[...] = gate
    up_ref[...] = up
    hidden = (gate * jax.nn.sigmoid(gate) * up).astype(bf16)
    for k in reversed(range(steps)):
        store_pair(parts[k], columns[k], (down_w,), (hidden,))


def backward_kernel(
    steps, held, gate_w, up_w, down_w, grad_sum, gate_ref, up_ref, gate_grad_ref, up_grad_ref, part
):
    columns = columns_of(steps, held.shape[2], 1)[-1]
    (hidden_grad,) = add_pair(held, columns, (down_w,), [grad_sum[...]])
    gate, up = gate_ref[...], up_ref[...]
    squash = jax.nn.sigmoid(gate)
    up_grad = (hidden_grad * (gate * squash)).astype(bf16)
    gate_grad = (hidden_grad * up * squash * (1.0 + gate * (1.0 - squash))).astype(bf16)
    gate_grad_ref[...] = gate_grad
    up_grad_ref[...] = up_grad
    store_pair(part, columns, (gate_w, up_w), (gate_grad, up_grad))


def late_kernel(steps, chain, *refs):
    parts = refs[-(steps - 1) :]
    rest = refs[: -(steps - 1)]
    weights, factors = rest[: len(rest) // 2], [f[...] for f in rest[len(rest) // 2 :]]
    columns = columns_of(steps, parts[0].shape[2], chain)
    for k in reversed(range(steps - 1)):
        store_pair(parts[k], columns[k], weights, factors)


def call(kernel, operands, shapes, flops, moved=4 << 20):
    return pl.pallas_call(
        kernel,
        out_shape=shapes,
        in_specs=[VMEM] * len(operands),
        out_specs=[VMEM] * len(shapes),
        compiler_params=pltpu.CompilerParams(vmem_limit_bytes=VMEM_LIMIT),
        cost_estimate=pl.CostEstimate(flops=flops, bytes_accessed=moved, transcendentals=0),
    )(*operands)


def sum_step(parts, arrived, step, chain):
    received = exchange(arrived, step, chain)
    return (parts[step - 1] + received.astype(f32)).astype(bf16)


def on_device(tokens, routes, route_weight, grad_out, w_gate, w_up, w_down):
    owners, steps = lax.axis_size("ep"), lax.axis_size("etp") // 2
    tok_rows, local_width = tokens.shape
    top_count = routes.shape[1]
    capacity = min(tok_rows, max(2, (3 * tok_rows * top_count + 2 * owners - 1) // (2 * owners)))
    slots = owners * capacity
    rows = 2 * slots
    inputs = (routes.T, route_weight.T, tokens, grad_out)
    send = pl.pallas_call(
        lambda *refs: dispatch_kernel(capacity, *refs),
        out_shape=jax.ShapeDtypeStruct((rows, local_width), bf16),
        in_specs=[HBM] * 4,
        out_specs=VMEM,
        scratch_shapes=[pltpu.VMEM(value.shape, value.dtype) for value in inputs]
        + [pltpu.SemaphoreType.DMA((4,))],
        compiler_params=pltpu.CompilerParams(vmem_limit_bytes=BIG),
    )(*inputs)
    recv = lax.all_to_all(
        send.reshape(owners, 2 * capacity, local_width), "ep", split_axis=0, concat_axis=0, tiled=True
    ).reshape(rows, local_width)
    half = jax.ShapeDtypeStruct((slots, local_width), bf16)
    token_rows, grad_rows = pl.pallas_call(
        lambda *refs: sort_kernel(capacity, *refs),
        out_shape=[half, half],
        in_specs=[VMEM, VMEM],
        out_specs=[VMEM] * 2,
        compiler_params=pltpu.CompilerParams(vmem_limit_bytes=VMEM_LIMIT),
    )(recv, w_down[0])
    token_next, grad_next = lax.optimization_barrier(
        (exchange(token_rows, 0, 0), exchange(grad_rows, 0, 1))
    )
    token_held = [jnp.stack([token_rows, token_next])]
    grad_held = [jnp.stack([grad_rows, grad_next])]
    for step in range(1, steps):
        token_held.append(exchange(token_held[-1], step, 0))
        grad_held.append(exchange(grad_held[-1], step, 1))
    gate_w, up_w, down_w = w_gate[0].T, w_up[0].T, w_down[0]
    hidden_width, width = down_w.shape
    total = jax.ShapeDtypeStruct((slots, hidden_width), f32)
    factor = jax.ShapeDtypeStruct((slots, hidden_width), bf16)
    leaving = jax.ShapeDtypeStruct((2, slots, local_width), bf16)
    kept = [jax.ShapeDtypeStruct((2, slots, local_width), f32)] * (steps - 1)
    flops = 2 * slots * hidden_width * width

    def early(*refs, chain):
        early_kernel(steps, chain, *refs)

    def late(*refs, chain):
        late_kernel(steps, chain, *refs)

    sums = call(
        functools.partial(early, chain=0), token_held[:-1] + [gate_w, up_w], [total] * 2, 2 * flops
    )
    (grad_sum,) = call(functools.partial(early, chain=1), grad_held[:-1] + [down_w], [total], flops)
    gate, up, *out_parts = call(
        functools.partial(forward_kernel, steps),
        [token_held[-1], gate_w, up_w, down_w, *sums],
        [total, total, *kept, leaving],
        flops,
    )
    gate_grad, up_grad, input_first = call(
        functools.partial(backward_kernel, steps),
        [grad_held[-1], gate_w, up_w, down_w, grad_sum, gate, up],
        [factor, factor, leaving],
        3 * flops,
        9 << 20,
    )
    input_parts = [
        *call(functools.partial(late, chain=1), [gate_w, up_w, gate_grad, up_grad], kept, 2 * flops),
        input_first,
    ]
    out_sum, input_sum = out_parts[-1], input_parts[-1]
    for step in reversed(range(1, steps)):
        out_sum = sum_step(out_parts, out_sum, step, 0)
        input_sum = sum_step(input_parts, input_sum, step, 1)
    unsorted = pl.pallas_call(
        lambda *refs: unsort_kernel(capacity, *refs),
        out_shape=jax.ShapeDtypeStruct((rows, local_width), bf16),
        in_specs=[VMEM] * 4,
        out_specs=VMEM,
        compiler_params=pltpu.CompilerParams(vmem_limit_bytes=VMEM_LIMIT),
    )(out_sum, exchange(out_sum[1], 0, 0), input_sum, exchange(input_sum[1], 0, 1))
    back = lax.all_to_all(
        unsorted.reshape(owners, 2 * capacity, local_width), "ep", split_axis=0, concat_axis=0, tiled=True
    ).reshape(rows, local_width)
    mine = jax.ShapeDtypeStruct((tok_rows, local_width), bf16)
    mixed, grad_tokens = pl.pallas_call(
        lambda *refs: combine_kernel(capacity, *refs),
        out_shape=[mine, mine],
        in_specs=[VMEM] * 3,
        out_specs=[VMEM] * 2,
        compiler_params=pltpu.CompilerParams(vmem_limit_bytes=VMEM_LIMIT),
    )(routes.T, route_weight.T, back)
    return (mixed, grad_tokens)


def solution(mesh):
    in_specs = (
        P("ep", "etp"),
        P("ep", None),
        P("ep", None),
        P("ep", "etp"),
        P("ep", None, "etp"),
        P("ep", None, "etp"),
        P("ep", "etp", None),
    )
    out_specs = (P("ep", "etp"), P("ep", "etp"))
    return jax.shard_map(
        on_device, mesh=mesh, in_specs=in_specs, out_specs=out_specs, check_vma=False
    )
```

```python
import functools

import jax
import jax.numpy as jnp
from jax import lax
from jax.experimental import pallas as pl
from jax.experimental.pallas import tpu as pltpu
from jax.sharding import PartitionSpec as P

bf16 = jnp.bfloat16
f32 = jnp.float32
VMEM = pl.BlockSpec(memory_space=pltpu.VMEM)
HBM = pl.BlockSpec(memory_space=pltpu.HBM)
VMEM_LIMIT = 16 * 1024 * 1024
BIG = 60 * 1024 * 1024


def dot_last(left, right):
    return lax.dot_general(left, right, (((1,), (1,)), ((), ())), preferred_element_type=f32)


def dot(left, right):
    return lax.dot_general(left, right, (((1,), (0,)), ((), ())), preferred_element_type=f32)


def split3(value):
    high = value.astype(bf16)
    rest = value - high.astype(f32)
    middle = rest.astype(bf16)
    return high, middle, (rest - middle.astype(f32)).astype(bf16)


def dot_first(left, right):
    return lax.dot_general(left, right, (((0,), (0,)), ((), ())), preferred_element_type=f32)


def travel_row(slot, kind, capacity):
    return lax.div(slot, capacity) * (2 * capacity) + kind * capacity + lax.rem(slot, capacity)


def picks(capacity, routes, weight, rows):
    shape = (rows, routes.shape[1])
    row = lax.broadcasted_iota(jnp.int32, shape, 0)
    owner = lax.div(row, 2 * capacity)
    named = jnp.zeros(shape, f32)
    scale = jnp.zeros(shape, f32)
    for k in range(routes.shape[0]):
        hit = routes[k : k + 1, :] == owner
        named = jnp.where(hit, 1.0, named)
        scale = jnp.where(hit, weight[k : k + 1, :], scale)
    square = (shape[1], shape[1])
    before = lax.broadcasted_iota(jnp.int32, square, 0) < lax.broadcasted_iota(jnp.int32, square, 1)
    earlier = dot(named.astype(bf16), before.astype(f32).astype(bf16))
    here = earlier == lax.rem(row, capacity).astype(f32)
    gradient = lax.rem(row, 2 * capacity) >= capacity
    return jnp.where(here, named, 0.0), jnp.where(here, scale, 0.0), gradient


def dispatch_kernel(capacity, *refs):
    outside, send, inside, sems = refs[:4], refs[4], refs[5:9], refs[9]
    copies = [pltpu.make_async_copy(outside[i], inside[i], sems.at[i]) for i in range(4)]
    for copy in copies:
        copy.start()
    for copy in copies:
        copy.wait()
    routes, weight, tokens, grads = inside
    pick, weighted, gradient = picks(capacity, routes, weight, send.shape[0])
    out = dot(jnp.where(gradient, 0.0, pick).astype(bf16), tokens[...])
    for part in split3(jnp.where(gradient, weighted, 0.0)):
        out = out + dot(part, grads[...])
    send[...] = out.astype(bf16)


def sort_kernel(capacity, recv, down_w, token_rows, grad_rows):
    del down_w
    rows = recv.shape[0]
    for kind, out in ((0, token_rows), (1, grad_rows)):
        shape = (rows // 2, rows)
        source = travel_row(lax.broadcasted_iota(jnp.int32, shape, 0), kind, capacity)
        place = (source == lax.broadcasted_iota(jnp.int32, shape, 1)).astype(f32).astype(bf16)
        out[...] = dot(place, recv[...]).astype(bf16)


def unsort_kernel(capacity, out_sum, out_last, input_sum, input_last, unsorted):
    rows = unsorted.shape[0]
    total = None
    for kind, held, last in ((0, out_sum, out_last), (1, input_sum, input_last)):
        local = (held[0].astype(f32) + last[...].astype(f32)).astype(bf16)
        shape = (rows, rows // 2)
        target = travel_row(lax.broadcasted_iota(jnp.int32, shape, 1), kind, capacity)
        place = (target == lax.broadcasted_iota(jnp.int32, shape, 0)).astype(f32).astype(bf16)
        now = dot(place, local)
        total = now if total is None else total + now
    unsorted[...] = total.astype(bf16)


def combine_kernel(capacity, routes, weight, back, mixed, grad_tokens):
    pick, weighted, gradient = picks(capacity, routes, weight, back.shape[0])
    rows = back[...]
    out = None
    for part in split3(jnp.where(gradient, 0.0, weighted)):
        now = dot_first(part, rows)
        out = now if out is None else out + now
    mixed[...] = out.astype(bf16)
    grad_tokens[...] = dot_first(jnp.where(gradient, pick, 0.0).astype(bf16), rows).astype(bf16)


def exchange(value, step, chain):
    size, owners = lax.axis_size("etp"), lax.axis_size("ep")
    pairs = []
    for y in range(size):
        for j in range(owners):
            sign = 1 if (y + 1 + step + chain) % 2 == 0 else -1
            pairs.append((y * owners + j, (y + sign) % size * owners + j))
    return lax.ppermute(value, ("etp", "ep"), pairs)


def columns_of(steps, width, chain):
    size = 2 * steps
    y = lax.axis_index("etp")
    sign = 1 - 2 * lax.rem(y + 1 + chain, 2)
    out = []
    for k in range(steps):
        turn = sign if k % 2 == 0 else -sign
        blocks = [lax.rem(y + turn * (k + b) + 2 * size, size) for b in (0, 1)]
        out.append([pl.ds(pl.multiple_of(block * width, width), width) for block in blocks])
    return out


def add_pair(held, columns, weights, totals):
    for b in (0, 1):
        now = [dot_last(held[b], weight[:, columns[b]]) for weight in weights]
        totals = now if totals is None else [x + y for x, y in zip(totals, now)]
    return totals


def store_pair(part, columns, weights, factors):
    for b in (0, 1):
        terms = [dot(f, weight[:, columns[b]]) for f, weight in zip(factors, weights)]
        part[b] = sum(terms[1:], terms[0]).astype(part.dtype)


def early_kernel(steps, chain, *refs):
    held, rest = refs[: steps - 1], refs[steps - 1 :]
    weights, totals = rest[: len(rest) // 2], rest[len(rest) // 2 :]
    columns = columns_of(steps, held[0].shape[2], chain)
    sums = None
    for k in range(steps - 1):
        sums = add_pair(held[k], columns[k], weights, sums)
    for total, value in zip(totals, sums):
        total[...] = value


def forward_kernel(steps, held, gate_w, up_w, down_w, gate_sum, up_sum, gate_ref, up_ref, *parts):
    columns = columns_of(steps, held.shape[2], 0)
    gate, up = add_pair(held, columns[-1], (gate_w, up_w), [gate_sum[...], up_sum[...]])
    gate_ref[...] = gate
    up_ref[...] = up
    hidden = (gate * jax.nn.sigmoid(gate) * up).astype(bf16)
    for k in reversed(range(steps)):
        store_pair(parts[k], columns[k], (down_w,), (hidden,))


def backward_kernel(
    steps, held, gate_w, up_w, down_w, grad_sum, gate_ref, up_ref, gate_grad_ref, up_grad_ref, part
):
    columns = columns_of(steps, held.shape[2], 1)[-1]
    (hidden_grad,) = add_pair(held, columns, (down_w,), [grad_sum[...]])
    gate, up = gate_ref[...], up_ref[...]
    squash = jax.nn.sigmoid(gate)
    up_grad = (hidden_grad * (gate * squash)).astype(bf16)
    gate_grad = (hidden_grad * up * squash * (1.0 + gate * (1.0 - squash))).astype(bf16)
    gate_grad_ref[...] = gate_grad
    up_grad_ref[...] = up_grad
    store_pair(part, columns, (gate_w, up_w), (gate_grad, up_grad))


def late_kernel(steps, chain, *refs):
    parts = refs[-(steps - 1) :]
    rest = refs[: -(steps - 1)]
    weights, factors = rest[: len(rest) // 2], [f[...] for f in rest[len(rest) // 2 :]]
    columns = columns_of(steps, parts[0].shape[2], chain)
    for k in reversed(range(steps - 1)):
        store_pair(parts[k], columns[k], weights, factors)


def call(kernel, operands, shapes, flops, moved=4 << 20):
    return pl.pallas_call(
        kernel,
        out_shape=shapes,
        in_specs=[VMEM] * len(operands),
        out_specs=[VMEM] * len(shapes),
        compiler_params=pltpu.CompilerParams(vmem_limit_bytes=VMEM_LIMIT),
        cost_estimate=pl.CostEstimate(flops=flops, bytes_accessed=moved, transcendentals=0),
    )(*operands)


def sum_step(parts, arrived, step, chain):
    received = exchange(arrived, step, chain)
    return (parts[step - 1] + received.astype(f32)).astype(bf16)


def on_device(tokens, routes, route_weight, grad_out, w_gate, w_up, w_down):
    owners, steps = lax.axis_size("ep"), lax.axis_size("etp") // 2
    tok_rows, local_width = tokens.shape
    top_count = routes.shape[1]
    capacity = min(tok_rows, max(2, (3 * tok_rows * top_count + 2 * owners - 1) // (2 * owners)))
    slots = owners * capacity
    rows = 2 * slots
    inputs = (routes.T, route_weight.T, tokens, grad_out)
    send = pl.pallas_call(
        lambda *refs: dispatch_kernel(capacity, *refs),
        out_shape=jax.ShapeDtypeStruct((rows, local_width), bf16),
        in_specs=[HBM] * 4,
        out_specs=VMEM,
        scratch_shapes=[pltpu.VMEM(value.shape, value.dtype) for value in inputs]
        + [pltpu.SemaphoreType.DMA((4,))],
        compiler_params=pltpu.CompilerParams(vmem_limit_bytes=BIG),
    )(*inputs)
    recv = lax.all_to_all(
        send.reshape(owners, 2 * capacity, local_width), "ep", split_axis=0, concat_axis=0, tiled=True
    ).reshape(rows, local_width)
    half = jax.ShapeDtypeStruct((slots, local_width), bf16)
    token_rows, grad_rows = pl.pallas_call(
        lambda *refs: sort_kernel(capacity, *refs),
        out_shape=[half, half],
        in_specs=[VMEM, VMEM],
        out_specs=[VMEM] * 2,
        compiler_params=pltpu.CompilerParams(vmem_limit_bytes=VMEM_LIMIT),
    )(recv, w_down[0])
    token_next, grad_next = lax.optimization_barrier(
        (exchange(token_rows, 0, 0), exchange(grad_rows, 0, 1))
    )
    token_held = [jnp.stack([token_rows, token_next])]
    grad_held = [jnp.stack([grad_rows, grad_next])]
    for step in range(1, steps):
        token_held.append(exchange(token_held[-1], step, 0))
        grad_held.append(exchange(grad_held[-1], step, 1))
    gate_w, up_w, down_w = w_gate[0].T, w_up[0].T, w_down[0]
    hidden_width, width = down_w.shape
    total = jax.ShapeDtypeStruct((slots, hidden_width), f32)
    factor = jax.ShapeDtypeStruct((slots, hidden_width), bf16)
    leaving = jax.ShapeDtypeStruct((2, slots, local_width), bf16)
    kept = [jax.ShapeDtypeStruct((2, slots, local_width), f32)] * (steps - 1)
    flops = 2 * slots * hidden_width * width

    def early(*refs, chain):
        early_kernel(steps, chain, *refs)

    def late(*refs, chain):
        late_kernel(steps, chain, *refs)

    sums = call(
        functools.partial(early, chain=0), token_held[:-1] + [gate_w, up_w], [total] * 2, 2 * flops
    )
    (grad_sum,) = call(functools.partial(early, chain=1), grad_held[:-1] + [down_w], [total], flops)
    gate, up, *out_parts = call(
        functools.partial(forward_kernel, steps),
        [token_held[-1], gate_w, up_w, down_w, *sums],
        [total, total, *kept, leaving],
        flops,
    )
    gate_grad, up_grad, input_first = call(
        functools.partial(backward_kernel, steps),
        [grad_held[-1], gate_w, up_w, down_w, grad_sum, gate, up],
        [factor, factor, leaving],
        3 * flops,
        9 << 20,
    )
    input_parts = [
        *call(functools.partial(late, chain=1), [gate_w, up_w, gate_grad, up_grad], kept, 2 * flops),
        input_first,
    ]
    out_sum, input_sum = out_parts[-1], input_parts[-1]
    for step in reversed(range(1, steps)):
        out_sum = sum_step(out_parts, out_sum, step, 0)
        input_sum = sum_step(input_parts, input_sum, step, 1)
    unsorted = pl.pallas_call(
        lambda *refs: unsort_kernel(capacity, *refs),
        out_shape=jax.ShapeDtypeStruct((rows, local_width), bf16),
        in_specs=[VMEM] * 4,
        out_specs=VMEM,
        compiler_params=pltpu.CompilerParams(vmem_limit_bytes=VMEM_LIMIT),
    )(out_sum, exchange(out_sum[1], 0, 0), input_sum, exchange(input_sum[1], 0, 1))
    back = lax.all_to_all(
        unsorted.reshape(owners, 2 * capacity, local_width), "ep", split_axis=0, concat_axis=0, tiled=True
    ).reshape(rows, local_width)
    mine = jax.ShapeDtypeStruct((tok_rows, local_width), bf16)
    mixed, grad_tokens = pl.pallas_call(
        lambda *refs: combine_kernel(capacity, *refs),
        out_shape=[mine, mine],
        in_specs=[VMEM] * 3,
        out_specs=[VMEM] * 2,
        compiler_params=pltpu.CompilerParams(vmem_limit_bytes=VMEM_LIMIT),
    )(routes.T, route_weight.T, back)
    return (mixed, grad_tokens)


def solution(mesh):
    in_specs = (
        P("ep", "etp"),
        P("ep", None),
        P("ep", None),
        P("ep", "etp"),
        P("ep", None, "etp"),
        P("ep", None, "etp"),
        P("ep", "etp", None),
    )
    out_specs = (P("ep", "etp"), P("ep", "etp"))
    return jax.shard_map(
        on_device, mesh=mesh, in_specs=in_specs, out_specs=out_specs, check_vma=False
    )
```

```python
import functools

import jax
import jax.numpy as jnp
from jax import lax
from jax.experimental import pallas as pl
from jax.experimental.pallas import tpu as pltpu
from jax.sharding import PartitionSpec as P

bf16 = jnp.bfloat16
f32 = jnp.float32
VMEM = pl.BlockSpec(memory_space=pltpu.VMEM)
HBM = pl.BlockSpec(memory_space=pltpu.HBM)
VMEM_LIMIT = 16 * 1024 * 1024
BIG = 60 * 1024 * 1024


def dot_last(left, right):
    return lax.dot_general(left, right, (((1,), (1,)), ((), ())), preferred_element_type=f32)


def dot(left, right):
    return lax.dot_general(left, right, (((1,), (0,)), ((), ())), preferred_element_type=f32)


def split3(value):
    high = value.astype(bf16)
    rest = value - high.astype(f32)
    middle = rest.astype(bf16)
    return high, middle, (rest - middle.astype(f32)).astype(bf16)


def dot_first(left, right):
    return lax.dot_general(left, right, (((0,), (0,)), ((), ())), preferred_element_type=f32)


def travel_row(slot, kind, capacity):
    return lax.div(slot, capacity) * (2 * capacity) + kind * capacity + lax.rem(slot, capacity)


def picks(capacity, routes, weight, rows):
    shape = (rows, routes.shape[1])
    row = lax.broadcasted_iota(jnp.int32, shape, 0)
    owner = lax.div(row, 2 * capacity)
    named = jnp.zeros(shape, f32)
    scale = jnp.zeros(shape, f32)
    for k in range(routes.shape[0]):
        hit = routes[k : k + 1, :] == owner
        named = jnp.where(hit, 1.0, named)
        scale = jnp.where(hit, weight[k : k + 1, :], scale)
    square = (shape[1], shape[1])
    before = lax.broadcasted_iota(jnp.int32, square, 0) < lax.broadcasted_iota(jnp.int32, square, 1)
    earlier = dot(named.astype(bf16), before.astype(f32).astype(bf16))
    here = earlier == lax.rem(row, capacity).astype(f32)
    gradient = lax.rem(row, 2 * capacity) >= capacity
    return jnp.where(here, named, 0.0), jnp.where(here, scale, 0.0), gradient


def dispatch_kernel(capacity, *refs):
    outside, send, inside, sems = refs[:4], refs[4], refs[5:9], refs[9]
    copies = [pltpu.make_async_copy(outside[i], inside[i], sems.at[i]) for i in range(4)]
    for copy in copies:
        copy.start()
    for copy in copies:
        copy.wait()
    routes, weight, tokens, grads = inside
    pick, weighted, gradient = picks(capacity, routes, weight, send.shape[0])
    out = dot(jnp.where(gradient, 0.0, pick).astype(bf16), tokens[...])
    for part in split3(jnp.where(gradient, weighted, 0.0)):
        out = out + dot(part, grads[...])
    send[...] = out.astype(bf16)


def sort_kernel(capacity, recv, down_w, token_rows, grad_rows):
    del down_w
    rows = recv.shape[0]
    for kind, out in ((0, token_rows), (1, grad_rows)):
        shape = (rows // 2, rows)
        source = travel_row(lax.broadcasted_iota(jnp.int32, shape, 0), kind, capacity)
        place = (source == lax.broadcasted_iota(jnp.int32, shape, 1)).astype(f32).astype(bf16)
        out[...] = dot(place, recv[...]).astype(bf16)


def unsort_kernel(capacity, out_sum, out_last, input_sum, input_last, unsorted):
    rows = unsorted.shape[0]
    total = None
    for kind, held, last in ((0, out_sum, out_last), (1, input_sum, input_last)):
        local = (held[0].astype(f32) + last[...].astype(f32)).astype(bf16)
        shape = (rows, rows // 2)
        target = travel_row(lax.broadcasted_iota(jnp.int32, shape, 1), kind, capacity)
        place = (target == lax.broadcasted_iota(jnp.int32, shape, 0)).astype(f32).astype(bf16)
        now = dot(place, local)
        total = now if total is None else total + now
    unsorted[...] = total.astype(bf16)


def combine_kernel(capacity, routes, weight, back, mixed, grad_tokens):
    pick, weighted, gradient = picks(capacity, routes, weight, back.shape[0])
    rows = back[...]
    out = None
    for part in split3(jnp.where(gradient, 0.0, weighted)):
        now = dot_first(part, rows)
        out = now if out is None else out + now
    mixed[...] = out.astype(bf16)
    grad_tokens[...] = dot_first(jnp.where(gradient, pick, 0.0).astype(bf16), rows).astype(bf16)


def exchange(value, step, chain):
    size, owners = lax.axis_size("etp"), lax.axis_size("ep")
    pairs = []
    for y in range(size):
        for j in range(owners):
            sign = 1 if (y + 1 + step + chain) % 2 == 0 else -1
            pairs.append((y * owners + j, (y + sign) % size * owners + j))
    return lax.ppermute(value, ("etp", "ep"), pairs)


def columns_of(steps, width, chain):
    size = 2 * steps
    y = lax.axis_index("etp")
    sign = 1 - 2 * lax.rem(y + 1 + chain, 2)
    out = []
    for k in range(steps):
        turn = sign if k % 2 == 0 else -sign
        blocks = [lax.rem(y + turn * (k + b) + 2 * size, size) for b in (0, 1)]
        out.append([pl.ds(pl.multiple_of(block * width, width), width) for block in blocks])
    return out


def add_pair(held, columns, weights, totals):
    for b in (0, 1):
        now = [dot_last(held[b], weight[:, columns[b]]) for weight in weights]
        totals = now if totals is None else [x + y for x, y in zip(totals, now)]
    return totals


def store_pair(part, columns, weights, factors):
    for b in (0, 1):
        terms = [dot(f, weight[:, columns[b]]) for f, weight in zip(factors, weights)]
        part[b] = sum(terms[1:], terms[0]).astype(part.dtype)


def early_kernel(steps, chain, *refs):
    held, rest = refs[: steps - 1], refs[steps - 1 :]
    weights, totals = rest[: len(rest) // 2], rest[len(rest) // 2 :]
    columns = columns_of(steps, held[0].shape[2], chain)
    sums = None
    for k in range(steps - 1):
        sums = add_pair(held[k], columns[k], weights, sums)
    for total, value in zip(totals, sums):
        total[...] = value


def forward_kernel(steps, held, gate_w, up_w, down_w, gate_sum, up_sum, gate_ref, up_ref, *parts):
    columns = columns_of(steps, held.shape[2], 0)
    gate, up = add_pair(held, columns[-1], (gate_w, up_w), [gate_sum[...], up_sum[...]])
    gate_ref[...] = gate
    up_ref[...] = up
    hidden = (gate * jax.nn.sigmoid(gate) * up).astype(bf16)
    for k in reversed(range(steps)):
        store_pair(parts[k], columns[k], (down_w,), (hidden,))


def backward_kernel(
    steps, held, gate_w, up_w, down_w, grad_sum, gate_ref, up_ref, gate_grad_ref, up_grad_ref, part
):
    columns = columns_of(steps, held.shape[2], 1)[-1]
    (hidden_grad,) = add_pair(held, columns, (down_w,), [grad_sum[...]])
    gate, up = gate_ref[...], up_ref[...]
    squash = jax.nn.sigmoid(gate)
    up_grad = (hidden_grad * (gate * squash)).astype(bf16)
    gate_grad = (hidden_grad * up * squash * (1.0 + gate * (1.0 - squash))).astype(bf16)
    gate_grad_ref[...] = gate_grad
    up_grad_ref[...] = up_grad
    store_pair(part, columns, (gate_w, up_w), (gate_grad, up_grad))


def late_kernel(steps, chain, *refs):
    parts = refs[-(steps - 1) :]
    rest = refs[: -(steps - 1)]
    weights, factors = rest[: len(rest) // 2], [f[...] for f in rest[len(rest) // 2 :]]
    columns = columns_of(steps, parts[0].shape[2], chain)
    for k in reversed(range(steps - 1)):
        store_pair(parts[k], columns[k], weights, factors)


def call(kernel, operands, shapes, flops, moved=4 << 20):
    return pl.pallas_call(
        kernel,
        out_shape=shapes,
        in_specs=[VMEM] * len(operands),
        out_specs=[VMEM] * len(shapes),
        compiler_params=pltpu.CompilerParams(vmem_limit_bytes=VMEM_LIMIT),
        cost_estimate=pl.CostEstimate(flops=flops, bytes_accessed=moved, transcendentals=0),
    )(*operands)


def sum_step(parts, arrived, step, chain):
    received = exchange(arrived, step, chain)
    return (parts[step - 1] + received.astype(f32)).astype(bf16)


def on_device(tokens, routes, route_weight, grad_out, w_gate, w_up, w_down):
    owners, steps = lax.axis_size("ep"), lax.axis_size("etp") // 2
    tok_rows, local_width = tokens.shape
    top_count = routes.shape[1]
    capacity = min(tok_rows, max(2, (3 * tok_rows * top_count + 2 * owners - 1) // (2 * owners)))
    slots = owners * capacity
    rows = 2 * slots
    inputs = (routes.T, route_weight.T, tokens, grad_out)
    send = pl.pallas_call(
        lambda *refs: dispatch_kernel(capacity, *refs),
        out_shape=jax.ShapeDtypeStruct((rows, local_width), bf16),
        in_specs=[HBM] * 4,
        out_specs=VMEM,
        scratch_shapes=[pltpu.VMEM(value.shape, value.dtype) for value in inputs]
        + [pltpu.SemaphoreType.DMA((4,))],
        compiler_params=pltpu.CompilerParams(vmem_limit_bytes=BIG),
    )(*inputs)
    recv = lax.all_to_all(
        send.reshape(owners, 2 * capacity, local_width), "ep", split_axis=0, concat_axis=0, tiled=True
    ).reshape(rows, local_width)
    half = jax.ShapeDtypeStruct((slots, local_width), bf16)
    token_rows, grad_rows = pl.pallas_call(
        lambda *refs: sort_kernel(capacity, *refs),
        out_shape=[half, half],
        in_specs=[VMEM, VMEM],
        out_specs=[VMEM] * 2,
        compiler_params=pltpu.CompilerParams(vmem_limit_bytes=VMEM_LIMIT),
    )(recv, w_down[0])
    grad_next, token_next = lax.optimization_barrier(
        (exchange(grad_rows, 0, 1), exchange(token_rows, 0, 0))
    )
    token_held = [jnp.stack([token_rows, token_next])]
    grad_held = [jnp.stack([grad_rows, grad_next])]
    for step in range(1, steps):
        token_held.append(exchange(token_held[-1], step, 0))
        grad_held.append(exchange(grad_held[-1], step, 1))
    gate_w, up_w, down_w = w_gate[0].T, w_up[0].T, w_down[0]
    hidden_width, width = down_w.shape
    total = jax.ShapeDtypeStruct((slots, hidden_width), f32)
    factor = jax.ShapeDtypeStruct((slots, hidden_width), bf16)
    leaving = jax.ShapeDtypeStruct((2, slots, local_width), bf16)
    kept = [jax.ShapeDtypeStruct((2, slots, local_width), f32)] * (steps - 1)
    flops = 2 * slots * hidden_width * width

    def early(*refs, chain):
        early_kernel(steps, chain, *refs)

    def late(*refs, chain):
        late_kernel(steps, chain, *refs)

    sums = call(
        functools.partial(early, chain=0), token_held[:-1] + [gate_w, up_w], [total] * 2, 2 * flops
    )
    (grad_sum,) = call(functools.partial(early, chain=1), grad_held[:-1] + [down_w], [total], flops)
    gate, up, *out_parts = call(
        functools.partial(forward_kernel, steps),
        [token_held[-1], gate_w, up_w, down_w, *sums],
        [total, total, *kept, leaving],
        flops,
    )
    gate_grad, up_grad, input_first = call(
        functools.partial(backward_kernel, steps),
        [grad_held[-1], gate_w, up_w, down_w, grad_sum, gate, up],
        [factor, factor, leaving],
        3 * flops,
        9 << 20,
    )
    input_parts = [
        *call(functools.partial(late, chain=1), [gate_w, up_w, gate_grad, up_grad], kept, 2 * flops),
        input_first,
    ]
    out_sum, input_sum = out_parts[-1], input_parts[-1]
    for step in reversed(range(1, steps)):
        out_sum = sum_step(out_parts, out_sum, step, 0)
        input_sum = sum_step(input_parts, input_sum, step, 1)
    unsorted = pl.pallas_call(
        lambda *refs: unsort_kernel(capacity, *refs),
        out_shape=jax.ShapeDtypeStruct((rows, local_width), bf16),
        in_specs=[VMEM] * 4,
        out_specs=VMEM,
        compiler_params=pltpu.CompilerParams(vmem_limit_bytes=VMEM_LIMIT),
    )(out_sum, exchange(out_sum[1], 0, 0), input_sum, exchange(input_sum[1], 0, 1))
    back = lax.all_to_all(
        unsorted.reshape(owners, 2 * capacity, local_width), "ep", split_axis=0, concat_axis=0, tiled=True
    ).reshape(rows, local_width)
    mine = jax.ShapeDtypeStruct((tok_rows, local_width), bf16)
    mixed, grad_tokens = pl.pallas_call(
        lambda *refs: combine_kernel(capacity, *refs),
        out_shape=[mine, mine],
        in_specs=[VMEM] * 3,
        out_specs=[VMEM] * 2,
        compiler_params=pltpu.CompilerParams(vmem_limit_bytes=VMEM_LIMIT),
    )(routes.T, route_weight.T, back)
    return (mixed, grad_tokens)


def solution(mesh):
    in_specs = (
        P("ep", "etp"),
        P("ep", None),
        P("ep", None),
        P("ep", "etp"),
        P("ep", None, "etp"),
        P("ep", None, "etp"),
        P("ep", "etp", None),
    )
    out_specs = (P("ep", "etp"), P("ep", "etp"))
    return jax.shard_map(
        on_device, mesh=mesh, in_specs=in_specs, out_specs=out_specs, check_vma=False
    )
```
